128 devices in a mesh: atm: 16 (over x, z), ocn: 8 (over y, core).
Axes of the slice: x: 4, y: 4, z: 4, core: 2. Of those that a mesh axis runs over, the one named last changes fastest.
Arguments:
- air_member_values: bfloat16 [16, 64, 256, 256], P('ocn', 'atm'), may hold values from -6 to 6
- marine_member_values: bfloat16 [16, 128, 256, 256], P('atm', 'ocn'), may hold values from -6 to 6
- air_neighbour_faces: int32 [64, 4], replicated, may hold values from 0 to 63, as said below
- marine_neighbour_faces: int32 [128, 4], replicated, may hold values from 0 to 127, as said below
- marine_spanned_quarter: int32 [128], replicated, may hold values from 0 to 255, as said below
- water_cell_indicator: int32 [128, 256], P('ocn'), may hold values 0 or 1
- initial_air_filter: bfloat16 [9, 256, 256], replicated, may hold values from -0.125 to 0.125
- initial_filter_offset: float32 [256], replicated, may hold values from -3 to 3
- later_air_filter: bfloat16 [9, 256, 256], replicated, may hold values from -0.125 to 0.125
- later_filter_offset: float32 [256], replicated, may hold values from -3 to 3
- air_to_exchange_matrix: bfloat16 [256, 16], replicated, may hold values from -0.375 to 0.375
- exchange_to_marine_matrix: bfloat16 [16, 256], replicated, may hold values from -1.5 to 1.5
- marine_wide_filter: bfloat16 [49, 256], replicated, may hold values from -0.875 to 0.875
- wide_filter_offset: float32 [256], replicated, may hold values from -3 to 3
- marine_rescale_factor: float32 [256], replicated, may hold values from 0.5 to 1.5
- hidden_entry_matrix: bfloat16 [256, 1024], replicated, may hold values from -0.375 to 0.375
- hidden_entry_offset: float32 [1024], replicated, may hold values from -3 to 3
- hidden_exit_matrix: bfloat16 [1024, 256], replicated, may hold values from -0.1875 to 0.1875
- marine_to_skin_matrix: bfloat16 [256, 16], replicated, may hold values from -0.375 to 0.375
- skin_to_air_matrix: bfloat16 [16, 256], replicated, may hold values from -1.5 to 1.5
Outputs:
- atm_next: bfloat16 [16, 64, 256, 256], P('ocn', 'atm')
- marine_values_advanced: bfloat16 [16, 128, 256, 256], P('atm', 'ocn')
The draws below stay inside these ranges and needn't reach their ends.
Inputs may be any that keep to these rules, and one draw needn't show every extreme that they name: `air_neighbour_faces`: entry s of row t is the tile beside t on side s (north, south, west, east); the north tile's south tile is t, and the west tile's east tile is t. `marine_neighbour_faces`: entry s of row t is the tile beside t on side s (north, south, west, east); the north tile's south tile is t, and the west tile's east tile is t. `marine_spanned_quarter`: Distinct; for each j exactly one of 2 * j and 2 * j + 1 appears.
All inputs are finite; a program needn't handle non-finite values. No bound on the sum of `water_cell_indicator` on one device may be relied on, other than what follows from the above.
Results may differ from the reference program's by a relative error of at most 0.01.
Values may be sent and summed in bfloat16 or wider, within the bound.
A program may use at most 128 MiB of HBM per device.

```python
import jax
import jax.numpy as jnp
from jax import lax

MODEL_FEATURES = 256
MLP_WIDTH = 1024
EXCHANGED_COUNT = 16
SIDE = 16
MEMBERS = 16
PIX = 256
HALF = 8
TILES_A = 64
TILES_O = 128


def torus_table(key, count):
    grid_rows = 4
    grid_cols = count // 4
    order = jax.random.permutation(key, count).astype(jnp.int32)
    place = jnp.zeros((count,), jnp.int32).at[order].set(jnp.arange(count, dtype=jnp.int32))
    row_at = place // grid_cols
    col_at = place % grid_cols
    north = order[(row_at - 1) % grid_rows * grid_cols + col_at]
    south = order[(row_at + 1) % grid_rows * grid_cols + col_at]
    west = order[row_at * grid_cols + (col_at - 1) % grid_cols]
    east = order[row_at * grid_cols + (col_at + 1) % grid_cols]
    return jnp.stack([north, south, west, east], axis=1).astype(jnp.int32)


def draw_air_neighbour_faces(key, part):
    key = jax.random.fold_in(key, 11)
    return torus_table(key, TILES_A)


def draw_marine_neighbour_faces(key, part):
    key = jax.random.fold_in(key, 12)
    return torus_table(key, TILES_O)


def draw_marine_spanned_quarter(key, part):
    key = jax.random.fold_in(key, 13)
    choose_bits = jax.random.randint(key, (TILES_O,), 0, 2).astype(jnp.int32)
    choose_bits = choose_bits.at[0].set(0).at[TILES_O - 1].set(1)
    quadrants = 2 * jnp.arange(TILES_O, dtype=jnp.int32) + choose_bits
    order = jax.random.permutation(jax.random.fold_in(key, 1), TILES_O).astype(jnp.int32)
    return quadrants[order]


def place_ends(entries, key, least, largest):
    index_at = [jax.random.randint(jax.random.fold_in(key, axis), (), 0, length) for axis, length in enumerate(entries.shape)]
    longest = entries.shape.index(max(entries.shape))
    neighbour = index_at[:longest] + [(index_at[longest] + 1) % entries.shape[longest]] + index_at[longest + 1:]
    return entries.at[tuple(index_at)].set(least).at[tuple(neighbour)].set(largest)


def block_levels(key, shape, pieces, smallest, largest):
    loudness, own = 1.0, jax.random.fold_in(key, 6)
    for position, parts in pieces:
        draws = jnp.exp(jax.random.uniform(jax.random.fold_in(own, position), (parts,), jnp.float32, smallest / len(pieces), largest / len(pieces)))
        loudness = loudness * jnp.repeat(draws, shape[position] // parts).reshape([-1 if axis == position else 1 for axis in range(len(shape))])
    return loudness


def scatter_about(stream_key, extent, deviation, reach, split=(), kind=jnp.bfloat16):
    values = jax.random.normal(stream_key, extent, jnp.float32) * deviation
    if len(split) > 0:
        values = block_levels(stream_key, extent, split, -0.22, 0.18) * values
    return jnp.clip(values, min=-reach, max=reach).astype(kind)


def setup_inputs(seed: int = 0) -> dict:
    key_list = jax.random.split(jax.random.key(seed), 21)
    air_member_values = scatter_about(key_list[0], (MEMBERS, TILES_A, PIX, MODEL_FEATURES), 1.0, 6.0, ((0, 8), (1, 16)))
    marine_member_values = scatter_about(key_list[1], (MEMBERS, TILES_O, PIX, MODEL_FEATURES), 1.0, 6.0, ((0, 16), (1, 8)))
    air_neighbour_faces = draw_air_neighbour_faces(jax.random.fold_in(key_list[20], 71), 0)
    marine_neighbour_faces = draw_marine_neighbour_faces(jax.random.fold_in(key_list[20], 71), 0)
    marine_spanned_quarter = draw_marine_spanned_quarter(jax.random.fold_in(key_list[20], 71), 0)
    water_cell_indicator = place_ends((jax.random.randint(key_list[5], (TILES_O, PIX), 0, 4) < 3).astype(jnp.int32), jax.random.fold_in(key_list[5], 1), 0, 1)
    initial_air_filter = scatter_about(key_list[6], (9, MODEL_FEATURES, MODEL_FEATURES), (9 * MODEL_FEATURES) ** -0.5, 0.125)
    initial_filter_offset = scatter_about(key_list[7], (MODEL_FEATURES,), 0.5, 3.0, (), jnp.float32)
    later_air_filter = scatter_about(key_list[8], (9, MODEL_FEATURES, MODEL_FEATURES), (9 * MODEL_FEATURES) ** -0.5, 0.125)
    later_filter_offset = scatter_about(key_list[9], (MODEL_FEATURES,), 0.5, 3.0, (), jnp.float32)
    air_to_exchange_matrix = scatter_about(key_list[10], (MODEL_FEATURES, EXCHANGED_COUNT), MODEL_FEATURES ** -0.5, 0.375)
    exchange_to_marine_matrix = scatter_about(key_list[11], (EXCHANGED_COUNT, MODEL_FEATURES), EXCHANGED_COUNT ** -0.5, 1.5)
    marine_wide_filter = scatter_about(key_list[12], (49, MODEL_FEATURES), 49 ** -0.5, 0.875)
    wide_filter_offset = scatter_about(key_list[13], (MODEL_FEATURES,), 0.5, 3.0, (), jnp.float32)
    marine_rescale_factor = jnp.clip(1.0 + 0.1 * jax.random.normal(key_list[14], (MODEL_FEATURES,), jnp.float32), 0.5, 1.5)
    hidden_entry_matrix = scatter_about(key_list[15], (MODEL_FEATURES, MLP_WIDTH), MODEL_FEATURES ** -0.5, 0.375)
    hidden_entry_offset = scatter_about(key_list[16], (MLP_WIDTH,), 0.5, 3.0, (), jnp.float32)
    hidden_exit_matrix = scatter_about(key_list[17], (MLP_WIDTH, MODEL_FEATURES), MLP_WIDTH ** -0.5, 0.1875)
    marine_to_skin_matrix = scatter_about(key_list[18], (MODEL_FEATURES, EXCHANGED_COUNT), MODEL_FEATURES ** -0.5, 0.375)
    skin_to_air_matrix = scatter_about(key_list[19], (EXCHANGED_COUNT, MODEL_FEATURES), EXCHANGED_COUNT ** -0.5, 1.5)
    return {"air_member_values": air_member_values, "marine_member_values": marine_member_values, "air_neighbour_faces": air_neighbour_faces, "marine_neighbour_faces": marine_neighbour_faces, "marine_spanned_quarter": marine_spanned_quarter, "water_cell_indicator": water_cell_indicator, "initial_air_filter": initial_air_filter, "initial_filter_offset": initial_filter_offset, "later_air_filter": later_air_filter, "later_filter_offset": later_filter_offset, "air_to_exchange_matrix": air_to_exchange_matrix, "exchange_to_marine_matrix": exchange_to_marine_matrix, "marine_wide_filter": marine_wide_filter, "wide_filter_offset": wide_filter_offset, "marine_rescale_factor": marine_rescale_factor, "hidden_entry_matrix": hidden_entry_matrix, "hidden_entry_offset": hidden_entry_offset, "hidden_exit_matrix": hidden_exit_matrix, "marine_to_skin_matrix": marine_to_skin_matrix, "skin_to_air_matrix": skin_to_air_matrix}


def pad_tiles(field, table, width):
    north = field[table[:, 0]][:, -width:, :, :]
    south = field[table[:, 1]][:, :width, :, :]
    west = field[table[:, 2]][:, :, -width:, :]
    east = field[table[:, 3]][:, :, :width, :]
    middle = jnp.concatenate([west, field, east], axis=2)
    blank = jnp.zeros((north.shape[0], width, width, north.shape[3]), field.dtype)
    upper = jnp.concatenate([blank, north, blank], axis=2)
    lower = jnp.concatenate([blank, south, blank], axis=2)
    return jnp.concatenate([upper, middle, lower], axis=1)

def atm_layer(state, table, kernel, bias):
    padded = pad_tiles(state, table, 1).astype(jnp.float32)
    total = jnp.zeros(state.shape, jnp.float32)
    for offset in range(9):
        row_shift, col_shift = divmod(offset, 3)
        window = padded[:, row_shift:row_shift + SIDE, col_shift:col_shift + SIDE, :]
        total = total + jnp.einsum('tpqc,cd->tpqd', window, kernel[offset].astype(jnp.float32))
    total = total + bias[None, None, None, :]
    return (state.astype(jnp.float32) + jax.nn.gelu(total)).astype(jnp.bfloat16)

def reference(air_member_values, marine_member_values, air_neighbour_faces, marine_neighbour_faces, marine_spanned_quarter, water_cell_indicator, initial_air_filter, initial_filter_offset, later_air_filter, later_filter_offset, air_to_exchange_matrix, exchange_to_marine_matrix, marine_wide_filter, wide_filter_offset, marine_rescale_factor, hidden_entry_matrix, hidden_entry_offset, hidden_exit_matrix, marine_to_skin_matrix, skin_to_air_matrix):
    number_format = jnp.float32

    def member(pair):
        atm_member, ocean_member = pair
        state = atm_member.reshape(TILES_A, SIDE, SIDE, MODEL_FEATURES)
        first = atm_layer(state, air_neighbour_faces, initial_air_filter, initial_filter_offset)
        flux = jnp.einsum('tpqc,cx->tpqx', first.astype(number_format), air_to_exchange_matrix.astype(number_format)).astype(jnp.bfloat16)
        quads = flux.reshape(TILES_A, 2, HALF, 2, HALF, EXCHANGED_COUNT).transpose(0, 1, 3, 2, 4, 5).reshape(4 * TILES_A, HALF, HALF, EXCHANGED_COUNT)
        chosen = quads[marine_spanned_quarter]
        fine = jnp.repeat(jnp.repeat(chosen, 2, axis=2), 2, axis=1)
        sea = water_cell_indicator.reshape(TILES_O, SIDE, SIDE, 1).astype(number_format)
        ocean = ocean_member.reshape(TILES_O, SIDE, SIDE, MODEL_FEATURES)
        forced = ocean.astype(number_format) + jnp.einsum('tpqf,fc->tpqc', fine.astype(number_format), exchange_to_marine_matrix.astype(number_format))
        masked = (forced * sea).astype(jnp.bfloat16)
        padded = pad_tiles(masked, marine_neighbour_faces, 3).astype(number_format)
        depth = jnp.zeros(forced.shape, number_format) + wide_filter_offset[None, None, None, :]
        for offset in range(49):
            row_shift, col_shift = divmod(offset, 7)
            window = padded[:, row_shift:row_shift + SIDE, col_shift:col_shift + SIDE, :]
            depth = depth + window * marine_wide_filter[offset].astype(number_format)[None, None, None, :]
        center = lax.optimization_barrier(jnp.mean(depth, axis=3, keepdims=True))
        spread = lax.optimization_barrier(jnp.mean((depth - center) ** 2, axis=3, keepdims=True))
        normed = ((depth - center) * lax.rsqrt(spread + 1e-06) * marine_rescale_factor[None, None, None, :]).astype(jnp.bfloat16)
        inner = jnp.einsum('tpqc,ch->tpqh', normed.astype(number_format), hidden_entry_matrix.astype(number_format)) + hidden_entry_offset[None, None, None, :]
        inner = jax.nn.gelu(inner).astype(jnp.bfloat16)
        outer = jnp.einsum('tpqh,hc->tpqc', inner.astype(number_format), hidden_exit_matrix.astype(number_format))
        marine_values_advanced = (sea * (forced + outer)).astype(jnp.bfloat16)
        skin_quantities = jnp.einsum('tpqc,cx->tpqx', marine_values_advanced.astype(number_format), marine_to_skin_matrix.astype(number_format)).astype(jnp.bfloat16)
        coarse = skin_quantities.astype(number_format).reshape(TILES_O, HALF, 2, HALF, 2, EXCHANGED_COUNT).mean(axis=(2, 4)).astype(jnp.bfloat16)
        field = jnp.zeros((4 * TILES_A, HALF, HALF, EXCHANGED_COUNT), jnp.bfloat16).at[marine_spanned_quarter].set(coarse)
        field = field.reshape(TILES_A, 2, 2, HALF, HALF, EXCHANGED_COUNT).transpose(0, 1, 3, 2, 4, 5).reshape(TILES_A, SIDE, SIDE, EXCHANGED_COUNT)
        second = (first.astype(number_format) + jnp.einsum('tpqf,fc->tpqc', field.astype(number_format), skin_to_air_matrix.astype(number_format))).astype(jnp.bfloat16)
        atm_next = atm_layer(second, air_neighbour_faces, later_air_filter, later_filter_offset)
        return (atm_next.reshape(TILES_A, PIX, MODEL_FEATURES), marine_values_advanced.reshape(TILES_O, PIX, MODEL_FEATURES))
    atm_next, marine_values_advanced = lax.map(member, (air_member_values, marine_member_values))
    return (atm_next, marine_values_advanced)
```

```python
import functools

import jax
import jax.numpy as jnp
import numpy as np
from jax import lax
from jax.experimental import pallas as pl
from jax.experimental.pallas import tpu as pltpu
from jax.sharding import PartitionSpec as P

BF = jnp.bfloat16
F32 = jnp.float32
MESH = pl.DeviceIdType.MESH
VMEM = pl.BlockSpec(memory_space=pltpu.VMEM)
SMEM = pl.BlockSpec(memory_space=pltpu.SMEM)
HBM = pl.BlockSpec(memory_space=pl.ANY)
C0 = 0.7978845608028654
C1 = C0 * 0.044715


def gelu(x):
    half = 0.5 * x
    return half + half * jnp.tanh(x * (C0 + C1 * (x * x)))


def dot(a, b):
    return jnp.dot(a, b, preferred_element_type=F32)


def dot_t(a, b):
    return lax.dot_general(a, b, (((0,), (0,)), ((), ())), preferred_element_type=F32)


def quarter_tables():
    split = np.zeros((256, 256), np.float32)
    join = np.zeros((256, 256), np.float32)
    for r in range(16):
        for q in range(16):
            a, b = r // 8, q // 8
            cell = (r % 8) * 8 + q % 8
            split[r * 16 + q, b * 128 + a * 64 + cell] = 1
            join[a * 128 + b * 64 + cell, r * 16 + q] = 1
    strip = np.zeros((4, 256, 128), np.float32)
    for c in range(16):
        for side, cell in enumerate((240 + c, c, c * 16 + 15, c * 16)):
            strip[side, :, side * 16 + c] = join[:, cell]
    up = np.zeros((128, 256), np.float32)
    for r in range(16):
        for q in range(16):
            up[(r // 2) * 8 + q // 2, r * 16 + q] = 1
    pick = np.zeros((4, 256, 256), np.float32)
    for j in range(3):
        for c in range(16):
            cells = ((13 + j) * 16 + c, j * 16 + c, c * 16 + 13 + j, c * 16 + j)
            for side, cell in enumerate(cells):
                pick[side, cell, side * 64 + j * 16 + c] = 1
    up_rim = np.einsum("qc,scd->sqd", up, pick)
    mean = np.zeros((2, 256, 128), np.float32)
    for r in range(16):
        for q in range(16):
            for h in range(2):
                mean[h, r * 16 + q, h * 64 + (r // 2) * 8 + q // 2] = 0.25
    cast = lambda v: jnp.asarray(v, BF)
    return (
        cast(split),
        cast(join),
        cast(strip.reshape(1024, 128)),
        cast(up),
        cast(up_rim.reshape(512, 256)),
        cast(pick.reshape(1024, 256)),
        cast(mean),
    )


def rims_kernel(marine, sea, rims, square):
    share = jnp.full((16, 256), 0.0625, BF)

    @pl.loop(0, 16)
    def _(t):
        row = jnp.broadcast_to(sea[pl.ds(t, 1), :].astype(F32), (16, 256)).astype(BF)
        wet = marine[t].astype(F32) * dot_t(row, share)
        rims[t, 0:48] = wet[0:48].astype(BF)
        rims[t, 48:96] = wet[208:256].astype(BF)
        square[...] = wet.reshape(16, 16, 256)
        for j in range(3):
            rims[t, 96 + 16 * j : 112 + 16 * j] = square[:, j, :].astype(BF)
            rims[t, 144 + 16 * j : 160 + 16 * j] = square[:, 13 + j, :].astype(BF)


def coordinates():
    a = lax.axis_index("atm")
    o = lax.axis_index("ocn")
    return a, o, lax.div(a, 4), lax.rem(a, 4)


def axis_partner(mm, phase, d):
    a, o, x, z = coordinates()
    if (mm + phase) % 2 == 0:
        place = lax.rem(z + d, 4)
        return (x * 4 + place, o), place
    place = lax.rem(x + d, 4)
    return (place * 4 + z, o), place


def rim_exchange(rd, tiles, nbr, square, g1, st, r2, send, recv):
    a, o, x, z = coordinates()

    def first_copy(mm, d):
        target, _ = axis_partner(mm, 0, d)
        _, here = axis_partner(mm, 0, 0)
        part = g1[rd][mm].at[here]
        return pltpu.make_async_remote_copy(
            src_ref=part, dst_ref=part, send_sem=send.at[rd, 0, mm, d - 1],
            recv_sem=recv.at[rd, 0, mm, d - 1], device_id=target, device_id_type=MESH)

    def second_copy(mm, d):
        target, _ = axis_partner(mm, 1, d)
        _, here = axis_partner(mm, 1, 0)
        return pltpu.make_async_remote_copy(
            src_ref=st.at[rd, mm, d - 1], dst_ref=r2[rd][mm].at[here],
            send_sem=send.at[rd, 1, mm, d - 1], recv_sem=recv.at[rd, 1, mm, d - 1],
            device_id=target, device_id_type=MESH)

    for mm in range(2):
        _, here = axis_partner(mm, 0, 0)

        @pl.loop(0, 4)
        def _(k):
            tile = tiles[mm, k]
            square[...] = tile.astype(F32).reshape(16, 16, 256)
            g1[rd][mm][here, k * 4] = tile[0:16]
            g1[rd][mm][here, k * 4 + 1] = tile[240:256]
            g1[rd][mm][here, k * 4 + 2] = square[:, 0, :].astype(BF)
            g1[rd][mm][here, k * 4 + 3] = square[:, 15, :].astype(BF)

        for d in (1, 3, 2):
            first_copy(mm, d).start()
    for mm in range(2):
        for d in (1, 2, 3):
            first_copy(mm, d).wait_recv()
        for d in (2, 1, 3, 0):
            (dest, _), place = axis_partner(mm, 1, d)

            @pl.loop(0, 16)
            def _(slot):
                n = nbr[dest * 16 + slot]
                owner = lax.div(n, 4)
                from_place = lax.rem(owner, 4) if mm == 0 else lax.div(owner, 4)
                side = lax.rem(slot, 4)
                kind = side + 1 - 2 * lax.rem(side, 2)
                strip = g1[rd][mm][from_place, lax.rem(n, 4) * 4 + kind]
                if d == 0:
                    r2[rd][mm][place, slot] = strip
                else:
                    st[rd, mm, d - 1, slot] = strip

            if d > 0:
                second_copy(mm, d).start()

    def finish():
        for mm in range(2):
            for d in (1, 2, 3):
                second_copy(mm, d).wait_recv()
        for mm in range(2):
            for d in (1, 2, 3):
                first_copy(mm, d).wait_send()
                second_copy(mm, d).wait_send()

    def strip_of(mm, slot):
        n = nbr[a * 16 + slot]
        owner = lax.div(n, 4)
        place = lax.div(owner, 4) if mm == 0 else lax.rem(owner, 4)
        return r2[rd][mm][place, slot]

    return finish, strip_of


def zero_corners(pad):
    blank = jnp.zeros((32, 256), F32)
    pad[0] = blank
    pad[17] = blank


def stage_tile(k, tile, strips, pad, shifted):
    pad[1:17, 8:24, :] = tile.astype(F32).reshape(16, 16, 256)
    pad[0, 8:24, :] = strips[0].astype(F32)
    pad[17, 8:24, :] = strips[1].astype(F32)
    pad[1:17, 7, :] = strips[2].astype(F32)
    pad[1:17, 24, :] = strips[3].astype(F32)
    for j in range(3):
        shifted[j, k] = pad[:, 7 + j : 23 + j, :].astype(BF).reshape(288, 256)


def convolve(shifted, filt, bias):
    total = None
    for offset in range(9):
        i, j = divmod(offset, 3)
        part = dot(shifted[j, :, i * 16 : i * 16 + 256, :].reshape(1024, 256), filt[offset])
        total = part if total is None else total + part
    return gelu(total + bias[...])


def greet(pairs_to, pairs_from, ring):
    barrier = pltpu.get_barrier_semaphore()
    a, o, x, z = coordinates()
    if ring:
        for mm in range(2):
            for d in (1, 2, 3):
                target, _ = axis_partner(mm, 0, d)
                pl.semaphore_signal(barrier, inc=1, device_id=target, device_id_type=MESH)

    @pl.loop(0, 16)
    def _(i):
        ta, to = pairs_from(i)

        @pl.when(jnp.logical_or(ta != a, to != o))
        def _():
            pl.semaphore_signal(barrier, inc=1, device_id=(ta, to), device_id_type=MESH)

    self_copy = jnp.where(lax.div(a, 2) == o, 1, 0)
    pl.semaphore_wait(barrier, (6 if ring else 0) + 16 - self_copy)


def air_kernel(air, filt, bias, flux_t, split, nbr, bits,
               first, halo, flux_all,
               square, pad, shifted, g00, g01, g10, g11, st, r00, r01, r10, r11,
               flux_own, flux_in, send, recv, fsend, frecv):
    g1 = ((g00, g01), (g10, g11))
    r2 = ((r00, r01), (r10, r11))
    a, o, x, z = coordinates()

    def flux_to(i):
        return 2 * o + lax.div(i, 8), lax.rem(i, 8)

    def flux_from(i):
        return i, lax.div(a, 2)

    greet(flux_to, flux_from, True)
    zero_corners(pad)
    finish, strip_of = rim_exchange(0, air, nbr, square, g1, st, r2, send, recv)
    finish()
    lane = lax.broadcasted_iota(jnp.int32, (16, 128), 1)
    for mm in range(2):
        @pl.loop(0, 4)
        def _(k):
            strips = [strip_of(mm, k * 4 + s) for s in range(4)]
            stage_tile(k, air[mm, k], strips, pad, shifted)

        first[mm] = (air[mm].astype(F32).reshape(1024, 256)
                     + convolve(shifted, filt, bias)).astype(BF).reshape(4, 256, 256)

        @pl.loop(0, 4)
        def _(k):
            flux = lax.dot_general(flux_t[...], first[mm, k], (((1,), (1,)), ((), ())),
                                   preferred_element_type=F32).astype(BF)
            quads = dot(flux, split[...])
            low = bits[a * 8 + k * 2]
            high = bits[a * 8 + k * 2 + 1]
            chosen = jnp.where(lane < 64, low, high)
            flux_own[mm, pl.ds(pl.multiple_of(k * 16, 16), 16)] = jnp.where(
                chosen == 1, quads[:, 128:], quads[:, :128]).astype(BF)

    def flux_copy(i):
        return pltpu.make_async_remote_copy(
            src_ref=flux_own.at[lax.div(i, 8)], dst_ref=flux_in.at[a],
            send_sem=fsend.at[i], recv_sem=frecv.at[a],
            device_id=flux_to(i), device_id_type=MESH)

    def arrival(i):
        return pltpu.make_async_remote_copy(
            src_ref=flux_own.at[0], dst_ref=flux_in.at[i],
            send_sem=fsend.at[i], recv_sem=frecv.at[i],
            device_id=flux_to(i), device_id_type=MESH)

    @pl.loop(0, 16)
    def _(i):
        ta, to = flux_to(i)
        mine = jnp.logical_and(ta == a, to == o)

        @pl.when(mine)
        def _():
            flux_in[a] = flux_own[lax.div(i, 8)]

        @pl.when(jnp.logical_not(mine))
        def _():
            flux_copy(i).start()

    finish, strip_of = rim_exchange(1, first, nbr, square, g1, st, r2, send, recv)

    @pl.loop(0, 16)
    def _(i):
        ta, to = flux_from(i)

        @pl.when(jnp.logical_or(ta != a, to != o))
        def _():
            arrival(i).wait_recv()

    flux_all[...] = flux_in[...]
    finish()
    for mm in range(2):
        @pl.loop(0, 16)
        def _(slot):
            halo[mm, slot] = strip_of(mm, slot)

    @pl.loop(0, 16)
    def _(i):
        ta, to = flux_to(i)

        @pl.when(jnp.logical_or(ta != a, to != o))
        def _():
            flux_copy(i).wait_send()


def ocean_kernel(marine, sea, sea_all, rims, flux_all, exchange, up, up_rim, pick, mean,
                 wide, wide_bias, gain, entry, entry_bias, leave, skin_t, nbr, quarter,
                 advanced, coarse,
                 strips, sems, fluxes, rim_flux, fine, fine_rim, rim_sea, rim_wet, wet32,
                 pad, depth, forced_all, normed_all):
    o = lax.axis_index("ocn")
    base = o * 16

    def strip_copy(t, s):
        n = nbr[(base + t) * 4 + s]
        start = (1 - s if s < 2 else 5 - s) * 48
        return pltpu.make_async_copy(
            rims.at[n, pl.ds(start, 48)], strips.at[t, s], sems.at[t, s])

    @pl.loop(0, 16)
    def _(t):
        for s in range(4):
            strip_copy(t, s).start()

    wet32[...] = sea_all[...].astype(F32)
    lane = lax.broadcasted_iota(jnp.int32, (16, 128), 1)

    def quadrant(tile):
        q = quarter[tile]
        both = flux_all[lax.div(q, 4)].astype(F32)
        upper = lax.rem(lax.div(q, 2), 2)
        moved = jnp.where(upper == 1, pltpu.roll(both, 64, 1), both)
        return jnp.where(lane < 64, moved, 0.0).astype(BF)

    @pl.loop(0, 16)
    def _(t):
        rows = pl.ds(pl.multiple_of(t * 16, 16), 16)
        fluxes[rows, :] = quadrant(base + t)
        for s in range(4):
            n = nbr[(base + t) * 4 + s]
            rim_flux[rows, s * 128 : (s + 1) * 128] = quadrant(n)
            rim_sea[pl.ds(t, 1), s * 256 : (s + 1) * 256] = wet32[pl.ds(n, 1), :]

    fine[...] = dot(fluxes[...], up[...]).astype(BF)
    fine_rim[...] = dot(rim_flux[...], up_rim[...])
    rim_wet[...] = dot(rim_sea[...].astype(BF), pick[...])
    share = jnp.full((16, 256), 0.0625, BF)
    pad[...] = jnp.zeros(pad.shape, F32)

    @pl.loop(0, 16)
    def _(t):
        rows = pl.ds(pl.multiple_of(t * 16, 16), 16)
        row = jnp.broadcast_to(sea[pl.ds(t, 1), :].astype(F32), (16, 256)).astype(BF)
        wet = dot_t(row, share)
        forced = marine[t].astype(F32) + dot_t(fine[rows, :], exchange[...])
        forced_all[t] = forced
        pad[3:19, 8:24, :] = (forced * wet).astype(BF).astype(F32).reshape(16, 16, 256)
        rim_in = (fine_rim[rows, :] * rim_wet[pl.ds(t, 1), :]).astype(BF)
        extra = dot_t(rim_in, exchange[...])
        for s in range(4):
            strip_copy(t, s).wait()

        def strip(s):
            value = strips[t, s].astype(F32) + extra[s * 64 : s * 64 + 48]
            return value.astype(BF).astype(F32)

        pad[0:3, 8:24, :] = strip(0).reshape(3, 16, 256)
        pad[19:22, 8:24, :] = strip(1).reshape(3, 16, 256)
        west = strip(2)
        east = strip(3)
        for j in range(3):
            pad[3:19, 5 + j, :] = west[16 * j : 16 * j + 16]
            pad[3:19, 24 + j, :] = east[16 * j : 16 * j + 16]
        for g in range(2):
            lanes = slice(g * 128, g * 128 + 128)
            for top in (0, 8):
                total = jnp.broadcast_to(wide_bias[:, lanes].reshape(1, 1, 128), (8, 16, 128))
                for j in range(7):
                    cols = pad[top : top + 14, 5 + j : 21 + j, lanes]
                    for i in range(7):
                        weight = wide[pl.ds(i * 7 + j, 1), lanes].reshape(1, 1, 128)
                        total = total + cols[i : i + 8] * weight
                depth[top * 16 : top * 16 + 128, lanes] = total.reshape(128, 128)
        value = depth[...]
        center = jnp.mean(value, axis=1, keepdims=True)
        value = value - center
        spread = jnp.mean(value * value, axis=1, keepdims=True)
        normed_all[t] = (value * lax.rsqrt(spread + 1e-6) * gain[...]).astype(BF)

    @pl.loop(0, 8)
    def _(p):
        two = pl.ds(p * 2, 2)
        inner = dot(normed_all[two].reshape(512, 256), entry[...]) + entry_bias[...]
        outer = dot(gelu(inner).astype(BF), leave[...])
        pair = jnp.zeros((16, 128), F32)
        for h in range(2):
            t = p * 2 + h
            row = jnp.broadcast_to(sea[pl.ds(t, 1), :].astype(F32), (16, 256)).astype(BF)
            wet = dot_t(row, share)
            result = (wet * (forced_all[t] + outer[h * 256 : h * 256 + 256])).astype(BF)
            advanced[t] = result
            surface = lax.dot_general(skin_t[...], result, (((1,), (1,)), ((), ())),
                                      preferred_element_type=F32).astype(BF)
            pair = pair + dot(surface, mean[h])
        coarse[p] = pair.astype(BF)


def return_kernel(coarse, first, halo, filt, bias, back, join, strip_sel, nbr, inverse, bits,
                  result,
                  held, pad, shifted, second, centre_q, rim_q, centre, rim, send, recv):
    a, o, x, z = coordinates()

    def skin_to(i):
        return i, lax.div(a, 2)

    def skin_from(i):
        return 2 * o + lax.div(i, 8), lax.rem(i, 8)

    greet(skin_to, skin_from, False)

    def skin_copy(i):
        return pltpu.make_async_remote_copy(
            src_ref=coarse, dst_ref=held.at[lax.rem(a, 2), o],
            send_sem=send.at[i], recv_sem=recv.at[lax.rem(a, 2) * 8 + o],
            device_id=skin_to(i), device_id_type=MESH)

    def arrival(i):
        return pltpu.make_async_remote_copy(
            src_ref=coarse, dst_ref=held.at[lax.div(i, 8), lax.rem(i, 8)],
            send_sem=send.at[i], recv_sem=recv.at[i],
            device_id=skin_to(i), device_id_type=MESH)

    @pl.loop(0, 16)
    def _(i):
        ta, to = skin_to(i)
        mine = jnp.logical_and(ta == a, to == o)

        @pl.when(mine)
        def _():
            held[lax.rem(a, 2), o] = coarse[...]

        @pl.when(jnp.logical_not(mine))
        def _():
            skin_copy(i).start()

    zero_corners(pad)

    @pl.loop(0, 16)
    def _(i):
        ta, to = skin_from(i)

        @pl.when(jnp.logical_or(ta != a, to != o))
        def _():
            arrival(i).wait_recv()

    lane = lax.broadcasted_iota(jnp.int32, (16, 128), 1)

    def half(mm, j):
        s = inverse[j]
        b = bits[j]
        both = held[mm, lax.div(s, 16), lax.div(lax.rem(s, 16), 2)].astype(F32)
        moved = jnp.where(lax.rem(s, 2) == b, both, pltpu.roll(both, 64, 1))
        inside = jnp.where(lane < 64, 0, 1) == b
        return jnp.where(inside, moved, 0.0).astype(BF)

    for mm in range(2):
        @pl.loop(0, 4)
        def _(k):
            rows = pl.ds(pl.multiple_of(mm * 64 + k * 16, 16), 16)
            tile = a * 4 + k
            for h in range(2):
                centre_q[rows, h * 128 : h * 128 + 128] = half(mm, tile * 2 + h)
                for s in range(4):
                    n = nbr[tile * 4 + s]
                    at = s * 256 + h * 128
                    rim_q[rows, at : at + 128] = half(mm, n * 2 + h)

    centre[...] = dot(centre_q[...], join[...]).astype(BF)
    rim[...] = dot(rim_q[...], strip_sel[...]).astype(BF)
    for mm in range(2):
        @pl.loop(0, 4)
        def _(k):
            rows = pl.ds(pl.multiple_of(mm * 64 + k * 16, 16), 16)
            tile = (first[mm, k].astype(F32) + dot_t(centre[rows, :], back[...])).astype(BF)
            second[k] = tile
            extra = dot_t(rim[rows, :], back[...])
            strips = [
                (halo[mm, k * 4 + s].astype(F32) + extra[s * 16 : s * 16 + 16]).astype(BF)
                for s in range(4)
            ]
            stage_tile(k, tile, strips, pad, shifted)

        result[mm] = (second[...].astype(F32).reshape(1024, 256)
                      + convolve(shifted, filt, bias)).astype(BF).reshape(4, 256, 256)

    @pl.loop(0, 16)
    def _(i):
        ta, to = skin_to(i)

        @pl.when(jnp.logical_or(ta != a, to != o))
        def _():
            skin_copy(i).wait_send()


def on_device(
    air_member_values,
    marine_member_values,
    air_neighbour_faces,
    marine_neighbour_faces,
    marine_spanned_quarter,
    water_cell_indicator,
    initial_air_filter,
    initial_filter_offset,
    later_air_filter,
    later_filter_offset,
    air_to_exchange_matrix,
    exchange_to_marine_matrix,
    marine_wide_filter,
    wide_filter_offset,
    marine_rescale_factor,
    hidden_entry_matrix,
    hidden_entry_offset,
    hidden_exit_matrix,
    marine_to_skin_matrix,
    skin_to_air_matrix,
):
    split, join, strip_sel, up, up_rim, pick, mean = quarter_tables()
    limit = 56 * 1024 * 1024
    marine = marine_member_values.reshape(16, 256, 256)
    sea = water_cell_indicator
    rims = pl.pallas_call(
        rims_kernel,
        out_shape=jax.ShapeDtypeStruct((16, 192, 256), BF),
        in_specs=[VMEM, VMEM],
        out_specs=VMEM,
        scratch_shapes=[pltpu.VMEM((16, 16, 256), F32)],
        compiler_params=pltpu.CompilerParams(vmem_limit_bytes=limit),
    )(marine, sea)
    rims_all = lax.all_gather(rims, "ocn", axis=0, tiled=True)
    sea_all = lax.all_gather(sea.astype(BF), "ocn", axis=0, tiled=True)

    air_nbr = air_neighbour_faces.reshape(256)
    ocean_nbr = marine_neighbour_faces.reshape(512)
    pair = marine_spanned_quarter // 2
    match = pair[None, :] == jnp.arange(128, dtype=jnp.int32)[:, None]
    inverse = jnp.sum(jnp.where(match, jnp.arange(128, dtype=jnp.int32)[None, :], 0), axis=1)
    bits = jnp.sum(jnp.where(match, (marine_spanned_quarter % 2)[None, :], 0), axis=1)

    first, halo, flux_all = pl.pallas_call(
        air_kernel,
        out_shape=(
            jax.ShapeDtypeStruct((2, 4, 256, 256), BF),
            jax.ShapeDtypeStruct((2, 16, 16, 256), BF),
            jax.ShapeDtypeStruct((16, 64, 128), BF),
        ),
        in_specs=[VMEM] * 5 + [SMEM] * 2,
        out_specs=(VMEM, VMEM, VMEM),
        scratch_shapes=[
            pltpu.VMEM((16, 16, 256), F32),
            pltpu.VMEM((18, 32, 256), F32),
            pltpu.VMEM((3, 4, 288, 256), BF),
        ] + [pltpu.VMEM((4, 16, 16, 256), BF)] * 4 + [
            pltpu.VMEM((2, 2, 3, 16, 16, 256), BF),
        ] + [pltpu.VMEM((4, 16, 16, 256), BF)] * 4 + [
            pltpu.VMEM((2, 64, 128), BF),
            pltpu.VMEM((16, 64, 128), BF),
            pltpu.SemaphoreType.DMA((2, 2, 2, 3)),
            pltpu.SemaphoreType.DMA((2, 2, 2, 3)),
            pltpu.SemaphoreType.DMA((16,)),
            pltpu.SemaphoreType.DMA((16,)),
        ],
        compiler_params=pltpu.CompilerParams(
            collective_id=0, has_side_effects=True, vmem_limit_bytes=limit),
    )(air_member_values, initial_air_filter, initial_filter_offset.reshape(1, 256),
      air_to_exchange_matrix.T, split, air_nbr, bits)

    advanced, coarse = pl.pallas_call(
        ocean_kernel,
        out_shape=(
            jax.ShapeDtypeStruct((16, 256, 256), BF),
            jax.ShapeDtypeStruct((8, 16, 128), BF),
        ),
        in_specs=[VMEM, VMEM, VMEM, HBM] + [VMEM] * 13 + [SMEM] * 2,
        out_specs=(VMEM, VMEM),
        scratch_shapes=[
            pltpu.VMEM((16, 4, 48, 256), BF),
            pltpu.SemaphoreType.DMA((16, 4)),
            pltpu.VMEM((256, 128), BF),
            pltpu.VMEM((256, 512), BF),
            pltpu.VMEM((256, 256), BF),
            pltpu.VMEM((256, 256), F32),
            pltpu.VMEM((16, 1024), F32),
            pltpu.VMEM((16, 256), F32),
            pltpu.VMEM((128, 256), F32),
            pltpu.VMEM((22, 32, 256), F32),
            pltpu.VMEM((256, 256), F32),
            pltpu.VMEM((16, 256, 256), F32),
            pltpu.VMEM((16, 256, 256), BF),
        ],
        compiler_params=pltpu.CompilerParams(vmem_limit_bytes=limit),
    )(marine, sea, sea_all, rims_all, flux_all.reshape(64, 16, 128), exchange_to_marine_matrix,
      up, up_rim, pick, mean, marine_wide_filter.astype(F32), wide_filter_offset.reshape(1, 256),
      marine_rescale_factor.reshape(1, 256), hidden_entry_matrix,
      hidden_entry_offset.reshape(1, 1024), hidden_exit_matrix, marine_to_skin_matrix.T,
      ocean_nbr, marine_spanned_quarter)

    atm_next = pl.pallas_call(
        return_kernel,
        out_shape=jax.ShapeDtypeStruct((2, 4, 256, 256), BF),
        in_specs=[VMEM] * 8 + [SMEM] * 3,
        out_specs=VMEM,
        scratch_shapes=[
            pltpu.VMEM((2, 8, 8, 16, 128), BF),
            pltpu.VMEM((18, 32, 256), F32),
            pltpu.VMEM((3, 4, 288, 256), BF),
            pltpu.VMEM((4, 256, 256), BF),
            pltpu.VMEM((128, 256), BF),
            pltpu.VMEM((128, 1024), BF),
            pltpu.VMEM((128, 256), BF),
            pltpu.VMEM((128, 128), BF),
            pltpu.SemaphoreType.DMA((16,)),
            pltpu.SemaphoreType.DMA((16,)),
        ],
        compiler_params=pltpu.CompilerParams(
            collective_id=1, has_side_effects=True, vmem_limit_bytes=limit),
    )(coarse, first, halo, later_air_filter, later_filter_offset.reshape(1, 256),
      skin_to_air_matrix, join, strip_sel, air_nbr, inverse, bits)
    return atm_next, advanced.reshape(1, 16, 256, 256)


def solution(mesh):
    in_specs = (
        P("ocn", "atm", None, None),
        P("atm", "ocn", None, None),
        P(),
        P(),
        P(),
        P("ocn", None),
    ) + (P(),) * 14
    out_specs = (P("ocn", "atm", None, None), P("atm", "ocn", None, None))
    return jax.shard_map(
        on_device, mesh=mesh, in_specs=in_specs, out_specs=out_specs, check_vma=False
    )
```

```python
import jax
import jax.numpy as jnp
import numpy as np
from jax import lax
from jax.experimental import pallas as pl
from jax.experimental.pallas import tpu as pltpu
from jax.sharding import PartitionSpec as P

BF = jnp.bfloat16
F32 = jnp.float32
MESH = pl.DeviceIdType.MESH
VMEM = pl.BlockSpec(memory_space=pltpu.VMEM)
SMEM = pl.BlockSpec(memory_space=pltpu.SMEM)
HBM = pl.BlockSpec(memory_space=pl.ANY)
C0 = 0.7978845608028654
C1 = C0 * 0.044715


def gelu(x):
    half = 0.5 * x
    return half + half * jnp.tanh(x * (C0 + C1 * (x * x)))


def dot(a, b):
    return jnp.dot(a, b, preferred_element_type=F32)


def dot_t(a, b):
    return lax.dot_general(a, b, (((0,), (0,)), ((), ())), preferred_element_type=F32)


def cell_tables():
    split = np.zeros((256, 256), np.float32)
    join = np.zeros((256, 256), np.float32)
    for r in range(16):
        for q in range(16):
            a, b = r // 8, q // 8
            cell = (r % 8) * 8 + q % 8
            split[r * 16 + q, b * 128 + a * 64 + cell] = 1
            join[a * 128 + b * 64 + cell, r * 16 + q] = 1
    air_rim = np.zeros((64, 256), np.float32)
    for c in range(16):
        for kind, cell in enumerate((c, 240 + c, c * 16, c * 16 + 15)):
            air_rim[kind * 16 + c, cell] = 1
    ocean_rim = np.zeros((192, 256), np.float32)
    for j in range(3):
        for c in range(16):
            cells = (j * 16 + c, (13 + j) * 16 + c, c * 16 + j, c * 16 + 13 + j)
            for kind, cell in enumerate(cells):
                ocean_rim[kind * 48 + j * 16 + c, cell] = 1
    strip = np.zeros((4, 256, 128), np.float32)
    for c in range(16):
        for side, cell in enumerate((240 + c, c, c * 16 + 15, c * 16)):
            strip[side, :, side * 16 + c] = join[:, cell]
    up = np.zeros((128, 256), np.float32)
    for r in range(16):
        for q in range(16):
            up[(r // 2) * 8 + q // 2, r * 16 + q] = 1
    pick = np.zeros((4, 256, 256), np.float32)
    for j in range(3):
        for c in range(16):
            cells = ((13 + j) * 16 + c, j * 16 + c, c * 16 + 13 + j, c * 16 + j)
            for side, cell in enumerate(cells):
                pick[side, cell, side * 64 + j * 16 + c] = 1
    up_rim = np.einsum("qc,scd->sqd", up, pick)
    shift = np.zeros((512, 7, 384), np.float32)
    for j in range(7):
        for q in range(16):
            col = q + j
            for r in range(22):
                at = r * 16 + q
                if 3 <= r < 19 and 3 <= col < 19:
                    shift[(r - 3) * 16 + col - 3, j, at] = 1
                elif 3 <= col < 19:
                    side, k = (0, r) if r < 3 else (1, r - 19)
                    shift[256 + side * 64 + k * 16 + col - 3, j, at] = 1
                elif 3 <= r < 19:
                    side, k = (2, col) if col < 3 else (3, col - 19)
                    shift[256 + side * 64 + k * 16 + r - 3, j, at] = 1
    mean = np.zeros((2, 256, 128), np.float32)
    for r in range(16):
        for q in range(16):
            for h in range(2):
                mean[h, r * 16 + q, h * 64 + (r // 2) * 8 + q // 2] = 0.25
    tables = (
        split,
        join,
        air_rim,
        ocean_rim,
        strip.reshape(1024, 128),
        up,
        up_rim.reshape(512, 256),
        pick.reshape(1024, 256),
        shift.reshape(512, 2688),
        mean,
    )
    return tuple(jnp.asarray(table, BF) for table in tables)


def coordinates():
    a = lax.axis_index("atm")
    o = lax.axis_index("ocn")
    return a, o, lax.div(a, 4), lax.rem(a, 4)


def axis_partner(mm, phase, d):
    a, o, x, z = coordinates()
    if (mm + phase) % 2 == 0:
        place = lax.rem(z + d, 4)
        return (x * 4 + place, o), place
    place = lax.rem(x + d, 4)
    return (place * 4 + z, o), place


def coupling_partner(k):
    a, o, x, z = coordinates()
    return 2 * o + k, lax.div(a, 2)


def is_me(k):
    a, o, x, z = coordinates()
    return jnp.logical_and(lax.div(a, 2) == o, lax.rem(a, 2) == k)


def remote(src, dst, send, recv, target):
    return pltpu.make_async_remote_copy(
        src_ref=src, dst_ref=dst, send_sem=send, recv_sem=recv,
        device_id=target, device_id_type=MESH)


def greet():
    barrier = pltpu.get_barrier_semaphore()
    a, o, x, z = coordinates()

    def signal(target):
        pl.semaphore_signal(barrier, inc=1, device_id=target, device_id_type=MESH)

    for d in (1, 2, 3):
        for mm in range(2):
            signal(axis_partner(mm, 0, d)[0])
    for d in range(1, 8):
        signal((a, lax.rem(o + d, 8)))
    for k in range(2):
        @pl.when(jnp.logical_not(is_me(k)))
        def _():
            signal(coupling_partner(k))


def await_greetings():
    a, o, x, z = coordinates()
    pl.semaphore_wait(pltpu.get_barrier_semaphore(), 15 - jnp.where(lax.div(a, 2) == o, 1, 0))


def rim_exchange(rd, tiles, nbr, air_rim, g1, st, r2, send, recv):
    a, o, x, z = coordinates()

    def first_copy(mm, d):
        here = axis_partner(mm, 0, 0)[1]
        part = g1[rd][mm].at[here]
        return remote(part, part, send.at[rd, 0, mm, d - 1], recv.at[rd, 0, mm, d - 1],
                      axis_partner(mm, 0, d)[0])

    def second_copy(mm, d):
        here = axis_partner(mm, 1, 0)[1]
        return remote(st.at[rd, mm, d - 1], r2[rd][mm].at[here], send.at[rd, 1, mm, d - 1],
                      recv.at[rd, 1, mm, d - 1], axis_partner(mm, 1, d)[0])

    def begin(mm):
        here = axis_partner(mm, 0, 0)[1]

        @pl.loop(0, 4)
        def _(k):
            rims = dot(air_rim[...], tiles[mm, k]).astype(BF).reshape(4, 16, 256)
            g1[rd][mm][here, pl.ds(k * 4, 4)] = rims

    def send_first(mm):
        for d in (1, 3, 2):
            first_copy(mm, d).start()

    def middle():
        for mm in range(2):
            for d in (1, 2, 3):
                first_copy(mm, d).wait_recv()
            for d in (2, 1, 3, 0):
                (dest, _), place = axis_partner(mm, 1, d)

                @pl.loop(0, 16, unroll=4)
                def _(slot):
                    n = nbr[lax.rem(slot, 4), dest * 4 + lax.div(slot, 4)]
                    owner = lax.div(n, 4)
                    from_place = lax.rem(owner, 4) if mm == 0 else lax.div(owner, 4)
                    side = lax.rem(slot, 4)
                    kind = side + 1 - 2 * lax.rem(side, 2)
                    strip = g1[rd][mm][from_place, lax.rem(n, 4) * 4 + kind]
                    if d == 0:
                        r2[rd][mm][place, slot] = strip
                    else:
                        st[rd, mm, d - 1, slot] = strip

                if d > 0:
                    second_copy(mm, d).start()

    def finish():
        for mm in range(2):
            for d in (1, 2, 3):
                second_copy(mm, d).wait_recv()
        for mm in range(2):
            for d in (1, 2, 3):
                first_copy(mm, d).wait_send()
                second_copy(mm, d).wait_send()

    def strip_of(mm, slot):
        n = nbr[lax.rem(slot, 4), a * 4 + lax.div(slot, 4)]
        owner = lax.div(n, 4)
        place = lax.div(owner, 4) if mm == 0 else lax.rem(owner, 4)
        return r2[rd][mm][place, slot]

    return begin, middle, finish, strip_of, send_first


def stage_tile(k, tile, strips, pad, shifted):
    pad[1:17, 8:24, :] = tile.astype(F32).reshape(16, 16, 256)
    pad[0, 8:24, :] = strips[0].astype(F32)
    pad[17, 8:24, :] = strips[1].astype(F32)
    pad[1:17, 7, :] = strips[2].astype(F32)
    pad[1:17, 24, :] = strips[3].astype(F32)
    for j in range(3):
        shifted[j, k] = pad[:, 7 + j : 23 + j, :].astype(BF).reshape(288, 256)


def convolve(shifted, filt, bias):
    total = None
    for offset in range(9):
        i, j = divmod(offset, 3)
        part = dot(shifted[j, :, i * 16 : i * 16 + 256, :].reshape(1024, 256), filt[offset])
        total = part if total is None else total + part
    return gelu(total + bias[...])


def interior(tile, wide, bias, pad, moved, depth):
    pad[:, 8:24, :] = tile
    for j in range(7):
        moved[j] = pad[:, 5 + j : 21 + j, :]
    for g in range(2):
        lanes = slice(g * 128, g * 128 + 128)
        start = jnp.broadcast_to(bias[:, lanes], (8, 128))
        for c in (0, 8):
            total = [start] * 16
            for j in range(7):
                rows = [moved[j, r, c : c + 8, lanes] for r in range(16)]
                weights = [wide[i * 7 + j, :, lanes] for i in range(7)]
                for p in range(16):
                    for i in range(7):
                        if 0 <= p + i - 3 < 16:
                            total[p] = total[p] + rows[p + i - 3] * weights[i]
            for p in range(16):
                depth[p, c : c + 8, lanes] = total[p]


def rim_sums(side, strip, wide, pad):
    pad[:, 8:24, :] = strip
    total = [None] * 3
    for shift in range(7):
        part = pad[:, 5 + shift : 21 + shift, :].reshape(3, 2, 8, 256)
        for place in range(3):
            for k in range(3):
                along = k - place if side in (0, 2) else 6 + k - place
                if not 0 <= along < 7 or (k < place) == (side in (0, 2)) and k != place:
                    continue
                i, j = (along, shift) if side < 2 else (shift, along)
                term = part[k] * wide[i * 7 + j][None]
                total[place] = term if total[place] is None else total[place] + term
    return [value.reshape(16, 256) for value in total]


def kernel(air, marine, sea, filt_a_far, bias_a, filt_b_far, bias_b, flux_t, exchange, wide_in,
           wide_bias, gain, entry_far, entry_bias, leave_far, skin_t, back,
           split, join, air_rim, ocean_rim, strip_sel, up, up_rim, pick, shift_far, mean,
           air_nbr, ocean_nbr, quarter, places,
           result, advanced,
           filt_a, filt_b, entry, leave, shift, fetch,
           first, pad_a, shifted, g00, g01, g10, g11, st, r00, r01, r10, r11,
           rims, sea_all, wet32, flux_own, flux_in, skin_in, back_out, back_in,
           wide, weights, pad_o, moved, pad_r, depth, forced,
           fluxes, rim_flux, rim_sea, cells, columns, im2col, centre_q, rim_q,
           asend, arecv, bsend, brecv, ssend, srecv, fsend, frecv, ksend, krecv):
    a, o, x, z = coordinates()
    g1 = ((g00, g01), (g10, g11))
    r2 = ((r00, r01), (r10, r11))
    right = (a, lax.rem(o + 2, 8))
    left = (a, lax.rem(o + 6, 8))
    twin = (a, o + 1 - 2 * lax.rem(o, 2))
    before = lax.rem(o + 6, 8)
    after = lax.rem(o + 2, 8)
    across = lax.rem(o + 4, 8)
    lane = lax.broadcasted_iota(jnp.int32, (16, 128), 1)
    share = jnp.full((16, 256), 0.0625, BF)

    def sea_columns(t):
        row = jnp.broadcast_to(sea[pl.ds(t, 1), :].astype(F32), (16, 256)).astype(BF)
        return dot_t(row, share)

    def rim_copy(block, half, target, n):
        part = rims.at[block, pl.ds(half * 8, 8)]
        return remote(part, part, bsend.at[n], brecv.at[n], target)

    def block_copy(block, n):
        return remote(rims.at[block], rims.at[block], bsend.at[n], brecv.at[n], twin)

    own_copies = [rim_copy(o, 0, right, 0), rim_copy(o, 1, left, 1),
                  rim_copy(o, 1, right, 2), rim_copy(o, 0, left, 3)]
    onward_right = rim_copy(before, 0, right, 4)
    onward_left = rim_copy(after, 1, left, 5)
    twin_copies = [block_copy(o, 6), block_copy(before, 7), block_copy(after, 8),
                   block_copy(across, 9)]

    def sea_copy(d):
        return remote(sea_all.at[o], sea_all.at[o], ssend.at[d - 1], srecv.at[d - 1],
                      (a, lax.rem(o + d, 8)))

    def flux_copy(d):
        part = flux_in.at[pl.ds(8 * o, 8)]
        return remote(part, part, fsend.at[d + 1], frecv.at[d + 1], (a, lax.rem(o + d, 8)))

    def skin_copy(d):
        return remote(skin_in.at[o], skin_in.at[o], ksend.at[d + 1], krecv.at[d + 1],
                      (a, lax.rem(o + d, 8)))

    def first_flux(k):
        return remote(flux_own.at[k], flux_in.at[pl.ds(4 * a, 4)], fsend.at[k], frecv.at[lax.rem(a, 2)],
                      coupling_partner(k))

    def last_skin(k):
        return remote(back_out.at[k], back_in.at[lax.rem(a, 2)], ksend.at[k],
                      krecv.at[lax.rem(a, 2)], coupling_partner(k))

    def unless_me(k, act):
        pl.when(jnp.logical_not(is_me(k)))(act)

    greet()
    fetches = [
        pltpu.make_async_copy(far, near, fetch.at[n])
        for n, (far, near) in enumerate((
            (filt_a_far, filt_a), (shift_far, shift), (entry_far, entry), (leave_far, leave),
            (filt_b_far, filt_b)))
    ]
    for copy in fetches:
        copy.start()
    air_first = rim_exchange(0, air, air_nbr, air_rim, g1, st, r2, asend, arecv)
    air_second = rim_exchange(1, first, air_nbr, air_rim, g1, st, r2, asend, arecv)
    air_first[0](0)
    air_first[0](1)
    sea_all[o] = sea[...].astype(F32).astype(BF)

    @pl.loop(0, 16)
    def _(t):
        wet = (marine[t].astype(F32) * sea_columns(t)).astype(BF)
        rims[o, t] = dot(ocean_rim[...], wet).astype(BF).reshape(4, 48, 256)

    await_greetings()
    air_first[4](0)
    air_first[4](1)
    for copy in own_copies:
        copy.start()
    twin_copies[0].start()
    for d in range(1, 8):
        sea_copy(d).start()

    spread_in = exchange[...].astype(F32)
    weights[...] = jnp.zeros(weights.shape, BF)
    for i in range(7):
        for j in range(7):
            row = wide_in[i * 7 + j : i * 7 + j + 1, :].astype(F32)
            wide[i * 7 + j] = jnp.broadcast_to(row, (8, 256))
            at = (i % 2) * 128 + j * 16
            weights[i // 2, at : at + 16, :] = (spread_in * row).astype(BF)
    pad_o[...] = jnp.zeros(pad_o.shape, F32)
    pad_r[...] = jnp.zeros(pad_r.shape, F32)
    pad_a[...] = jnp.zeros(pad_a.shape, F32)

    def interiors(low, high):
        @pl.loop(low, high)
        def _(t):
            tile = (marine[t].astype(F32) * sea_columns(t)).reshape(16, 16, 256)
            interior(tile, wide, wide_bias, pad_o, moved, depth.at[t])

    interiors(0, 5)
    air_first[1]()
    interiors(5, 11)
    air_first[2]()
    fetches[0].wait()

    for mm in range(2):
        @pl.loop(0, 4)
        def _(k):
            strips = [air_first[3](mm, k * 4 + s) for s in range(4)]
            stage_tile(k, air[mm, k], strips, pad_a, shifted)

        first[mm] = (air[mm].astype(F32).reshape(1024, 256)
                     + convolve(shifted, filt_a, bias_a)).astype(BF).reshape(4, 256, 256)

        @pl.loop(0, 4)
        def _(k):
            flux = lax.dot_general(flux_t[...], first[mm, k], (((1,), (1,)), ((), ())),
                                   preferred_element_type=F32).astype(BF)
            quads = dot(flux, split[...])
            low = lax.rem(places[a * 8 + k * 2], 2)
            high = lax.rem(places[a * 8 + k * 2 + 1], 2)
            chosen = jnp.where(lane < 64, low, high)
            flux_own[mm, k] = jnp.where(
                chosen == 1, quads[:, 128:], quads[:, :128]).astype(BF)

        unless_me(mm, lambda: first_flux(mm).start())

        @pl.when(is_me(mm))
        def _():
            flux_in[pl.ds(4 * a, 4)] = flux_own[mm]

        air_second[0](mm)
        air_second[4](mm)

    own_copies[0].wait_recv()
    onward_right.start()
    own_copies[1].wait_recv()
    onward_left.start()

    interiors(11, 14)
    for k in range(2):
        def arrival():
            remote(flux_own.at[0], flux_in.at[pl.ds(8 * o + 4 * k, 4)], fsend.at[k], frecv.at[k],
                   coupling_partner(k)).wait_recv()
        unless_me(k, arrival)
    for d in range(1, 8):
        flux_copy(d).start()
    interiors(14, 16)
    air_second[1]()
    for d in range(1, 8):
        sea_copy(d).wait_recv()
    wet32[...] = sea_all[...].astype(F32).reshape(128, 1, 256)
    for d in range(1, 8):
        flux_copy(d).wait_recv()

    def quadrant(tile):
        q = quarter[tile]
        both = flux_in[lax.div(q, 4)].astype(F32)
        upper = lax.rem(lax.div(q, 2), 2)
        turned = jnp.where(upper == 1, pltpu.roll(both, 64, 1), both)
        return jnp.where(lane < 64, turned, 0.0).astype(BF)

    @pl.loop(0, 16)
    def _(t):
        rows = pl.ds(pl.multiple_of(t * 16, 16), 16)
        fluxes[rows, :] = quadrant(o * 16 + t)
        for s in range(4):
            n = ocean_nbr[s, o * 16 + t]
            rim_flux[rows, s * 128 : (s + 1) * 128] = quadrant(n)
            rim_sea[pl.ds(t, 1), s * 256 : (s + 1) * 256] = wet32[n]

    fine = dot(fluxes[...], up[...])
    sea_here = jnp.broadcast_to(sea[...].astype(F32).reshape(16, 1, 256), (16, 16, 256))
    cells[:, 0:256] = (fine * sea_here.reshape(256, 256)).astype(BF)
    rim_wet = dot(rim_sea[...].astype(BF), pick[...])
    rim_wet = jnp.broadcast_to(rim_wet.reshape(16, 1, 256), (16, 16, 256)).reshape(256, 256)
    cells[:, 256:512] = (dot(rim_flux[...], up_rim[...]) * rim_wet).astype(BF)
    fine = fine.astype(BF)
    for t in range(16):
        forced[t] = (marine[t].astype(F32) + dot_t(fine[t * 16 : t * 16 + 16], exchange[...]))

    own_copies[2].wait_recv()
    twin_copies[1].start()
    own_copies[3].wait_recv()
    twin_copies[2].start()

    fetches[1].wait()
    columns[:, 112:128, :] = jnp.zeros((16, 16, 384), BF)
    for j in range(7):
        shifts = dot(cells[...], shift[:, j * 384 : j * 384 + 384]).astype(BF)
        columns[:, j * 16 : j * 16 + 16, :] = shifts.reshape(16, 16, 384)

    @pl.loop(0, 16)
    def _(t):
        turned = columns[t].astype(F32).T.astype(BF)
        im2col[t, :, 0:128] = turned
        im2col[t, 0:368, 128:256] = turned[16:384]
        im2col[t, 368:384, 128:256] = jnp.zeros((16, 128), BF)

    onward_right.wait_recv()
    onward_left.wait_recv()
    twin_copies[3].start()

    @pl.loop(0, 4)
    def _(p):
        four = pl.ds(p * 4, 4)
        total = depth[four].reshape(1024, 256)
        for i in range(4):
            total = total + dot(im2col[four, i * 32 : i * 32 + 256, :].reshape(1024, 256),
                                weights[i])
        depth[four] = total.reshape(4, 16, 16, 256)

    for copy in twin_copies:
        copy.wait_recv()

    @pl.loop(0, 16)
    def _(t):
        for s in range(4):
            n = ocean_nbr[s, o * 16 + t]
            kind = s + 1 - 2 * (s % 2)
            strip = rims[lax.div(n, 16), lax.rem(n, 16), kind]
            sums = rim_sums(s, strip.astype(F32).reshape(3, 16, 256), wide, pad_r)
            for place in range(3):
                if s < 2:
                    row = place + 13 * s
                    depth[t, row] = depth[t, row] + sums[place]
                else:
                    col = place + 13 * (s - 2)
                    depth[t, :, col, :] = depth[t, :, col, :] + sums[place]

    fetches[2].wait()
    fetches[3].wait()

    @pl.loop(0, 8)
    def _(p):
        two = pl.ds(p * 2, 2)
        value = depth[two].reshape(512, 256)
        value = value - jnp.mean(value, axis=1, keepdims=True)
        spread = jnp.mean(value * value, axis=1, keepdims=True)
        normed = (value * lax.rsqrt(spread + 1e-6) * gain[...]).astype(BF)
        inner = dot(normed, entry[...]) + entry_bias[...]
        outer = dot(gelu(inner).astype(BF), leave[...])
        pair = jnp.zeros((16, 128), F32)
        for h in range(2):
            t = p * 2 + h
            whole = forced[t] + outer[h * 256 : h * 256 + 256]
            done = (sea_columns(t) * whole).astype(BF)
            advanced[t] = done
            surface = lax.dot_general(skin_t[...], done, (((1,), (1,)), ((), ())),
                                      preferred_element_type=F32).astype(BF)
            pair = pair + dot(surface, mean[h])
        skin_in[o, p] = pair.astype(BF)

    for d in range(1, 8):
        skin_copy(d).start()
    air_second[2]()
    for d in range(1, 8):
        skin_copy(d).wait_recv()

    fetches[4].wait()

    def half(j):
        s = lax.div(places[j], 2)
        b = lax.rem(places[j], 2)
        both = skin_in[lax.div(s, 16), lax.div(lax.rem(s, 16), 2)].astype(F32)
        turned = jnp.where(lax.rem(s, 2) == b, both, pltpu.roll(both, 64, 1))
        inside = jnp.where(lane < 64, 0, 1) == b
        return jnp.where(inside, turned, 0.0).astype(BF)

    @pl.loop(0, 8)
    def _(k):
        rows = pl.ds(pl.multiple_of(k * 16, 16), 16)
        tile = o * 8 + k
        for h in range(2):
            centre_q[rows, h * 128 : h * 128 + 128] = half(tile * 2 + h)
            for s in range(4):
                n = air_nbr[s, tile]
                at = s * 256 + h * 128
                rim_q[rows, at : at + 128] = half(n * 2 + h)

    centre = dot(centre_q[...], join[...]).astype(BF)
    rim = dot(rim_q[...], strip_sel[...]).astype(BF)
    for k in range(2):
        back_out[k, :, 0:256] = centre[k * 64 : k * 64 + 64]
        back_out[k, :, 256:384] = rim[k * 64 : k * 64 + 64]
        unless_me(k, lambda: last_skin(k).start())

        @pl.when(is_me(k))
        def _():
            back_in[k] = back_out[k]

    for mm in range(2):
        def arrival():
            remote(back_out.at[0], back_in.at[mm], ksend.at[mm], krecv.at[mm],
                   coupling_partner(mm)).wait_recv()
        unless_me(mm, arrival)

        @pl.loop(0, 4)
        def _(k):
            rows = pl.ds(pl.multiple_of(k * 16, 16), 16)
            add = dot_t(back_in[mm, rows, 0:256], back[...])
            tile = (first[mm, k].astype(F32) + add).astype(BF)
            result[mm, k] = tile
            extra = dot_t(back_in[mm, rows, 256:384], back[...])
            strips = [
                (air_second[3](mm, k * 4 + s).astype(F32) + extra[s * 16 : s * 16 + 16]).astype(BF)
                for s in range(4)
            ]
            stage_tile(k, tile, strips, pad_a, shifted)

        result[mm] = (result[mm].astype(F32).reshape(1024, 256)
                      + convolve(shifted, filt_b, bias_b)).astype(BF).reshape(4, 256, 256)

    for copy in own_copies + [onward_right, onward_left] + twin_copies:
        copy.wait_send()
    for d in range(1, 8):
        sea_copy(d).wait_send()
        flux_copy(d).wait_send()
        skin_copy(d).wait_send()
    for k in range(2):
        unless_me(k, lambda: first_flux(k).wait_send())
        unless_me(k, lambda: last_skin(k).wait_send())


def on_device(
    air_member_values,
    marine_member_values,
    air_neighbour_faces,
    marine_neighbour_faces,
    marine_spanned_quarter,
    water_cell_indicator,
    initial_air_filter,
    initial_filter_offset,
    later_air_filter,
    later_filter_offset,
    air_to_exchange_matrix,
    exchange_to_marine_matrix,
    marine_wide_filter,
    wide_filter_offset,
    marine_rescale_factor,
    hidden_entry_matrix,
    hidden_entry_offset,
    hidden_exit_matrix,
    marine_to_skin_matrix,
    skin_to_air_matrix,
):
    index = lax.broadcasted_iota(jnp.int32, (128, 128), 0)
    tile = lax.broadcasted_iota(jnp.int32, (128, 128), 1)
    covered = jnp.broadcast_to(marine_spanned_quarter[None, :], (128, 128))
    code = jnp.where((covered >> 1) == index, 2 * tile + (covered & 1), 0)
    places = jnp.sum(code, axis=1)
    strips = pltpu.VMEM((4, 16, 16, 256), BF)
    dma = pltpu.SemaphoreType.DMA
    atm_next, advanced = pl.pallas_call(
        kernel,
        out_shape=(
            jax.ShapeDtypeStruct((2, 4, 256, 256), BF),
            jax.ShapeDtypeStruct((16, 256, 256), BF),
        ),
        in_specs=[VMEM] * 3 + [HBM, VMEM, HBM] + [VMEM] * 6 + [HBM, VMEM, HBM] + [VMEM] * 10
        + [HBM, VMEM] + [SMEM] * 4,
        out_specs=(VMEM, VMEM),
        scratch_shapes=[
            pltpu.VMEM((9, 256, 256), BF),
            pltpu.VMEM((9, 256, 256), BF),
            pltpu.VMEM((256, 1024), BF),
            pltpu.VMEM((1024, 256), BF),
            pltpu.VMEM((512, 2688), BF),
            dma((5,)),
            pltpu.VMEM((2, 4, 256, 256), BF),
            pltpu.VMEM((18, 32, 256), F32),
            pltpu.VMEM((3, 4, 288, 256), BF),
            strips, strips, strips, strips,
            pltpu.VMEM((2, 2, 3, 16, 16, 256), BF),
            strips, strips, strips, strips,
            pltpu.VMEM((8, 16, 4, 48, 256), BF),
            pltpu.VMEM((8, 16, 256), BF),
            pltpu.VMEM((128, 1, 256), F32),
            pltpu.VMEM((2, 4, 16, 128), BF),
            pltpu.VMEM((64, 16, 128), BF),
            pltpu.VMEM((8, 8, 16, 128), BF),
            pltpu.VMEM((2, 64, 384), BF),
            pltpu.VMEM((2, 64, 384), BF),
            pltpu.VMEM((49, 8, 256), F32),
            pltpu.VMEM((4, 256, 256), BF),
            pltpu.VMEM((16, 32, 256), F32),
            pltpu.VMEM((7, 16, 16, 256), F32),
            pltpu.VMEM((3, 32, 256), F32),
            pltpu.VMEM((16, 16, 16, 256), F32),
            pltpu.VMEM((16, 256, 256), F32),
            pltpu.VMEM((256, 128), BF),
            pltpu.VMEM((256, 512), BF),
            pltpu.VMEM((16, 1024), F32),
            pltpu.VMEM((256, 512), BF),
            pltpu.VMEM((16, 128, 384), BF),
            pltpu.VMEM((16, 384, 256), BF),
            pltpu.VMEM((128, 256), BF),
            pltpu.VMEM((128, 1024), BF),
            dma((2, 2, 2, 3)), dma((2, 2, 2, 3)),
            dma((10,)), dma((10,)),
            dma((7,)), dma((7,)),
            dma((9,)), dma((9,)),
            dma((9,)), dma((9,)),
        ],
        compiler_params=pltpu.CompilerParams(
            collective_id=0, has_side_effects=True, vmem_limit_bytes=60 * 1024 * 1024),
    )(
        air_member_values, marine_member_values.reshape(16, 256, 256), water_cell_indicator,
        initial_air_filter, initial_filter_offset.reshape(1, 256),
        later_air_filter, later_filter_offset.reshape(1, 256),
        air_to_exchange_matrix.T, exchange_to_marine_matrix, marine_wide_filter,
        wide_filter_offset.reshape(1, 256), marine_rescale_factor.reshape(1, 256),
        hidden_entry_matrix, hidden_entry_offset.reshape(1, 1024), hidden_exit_matrix,
        marine_to_skin_matrix.T, skin_to_air_matrix, *cell_tables(),
        air_neighbour_faces.T, marine_neighbour_faces.T, marine_spanned_quarter, places,
    )
    return atm_next, advanced.reshape(1, 16, 256, 256)


def solution(mesh):
    in_specs = (
        P("ocn", "atm", None, None),
        P("atm", "ocn", None, None),
        P(),
        P(),
        P(),
        P("ocn", None),
    ) + (P(),) * 14
    out_specs = (P("ocn", "atm", None, None), P("atm", "ocn", None, None))
    return jax.shard_map(
        on_device, mesh=mesh, in_specs=in_specs, out_specs=out_specs, check_vma=False
    )
```

```python
import jax
import jax.numpy as jnp
import numpy as np
from jax import lax
from jax.experimental import pallas as pl
from jax.experimental.pallas import tpu as pltpu
from jax.sharding import PartitionSpec as P

BF = jnp.bfloat16
F32 = jnp.float32
MESH = pl.DeviceIdType.MESH
VMEM = pl.BlockSpec(memory_space=pltpu.VMEM)
SMEM = pl.BlockSpec(memory_space=pltpu.SMEM)
HBM = pl.BlockSpec(memory_space=pl.ANY)
C0 = 0.7978845608028654
C1 = C0 * 0.044715


def gelu(x):
    half = 0.5 * x
    return half + half * jnp.tanh(x * (C0 + C1 * (x * x)))


def dot(a, b):
    return jnp.dot(a, b, preferred_element_type=F32)


def dot_t(a, b):
    return lax.dot_general(a, b, (((0,), (0,)), ((), ())), preferred_element_type=F32)


def cell_tables():
    split = np.zeros((256, 256), np.float32)
    join = np.zeros((256, 256), np.float32)
    for r in range(16):
        for q in range(16):
            a, b = r // 8, q // 8
            cell = (r % 8) * 8 + q % 8
            split[r * 16 + q, b * 128 + a * 64 + cell] = 1
            join[a * 128 + b * 64 + cell, r * 16 + q] = 1
    air_rim = np.zeros((64, 256), np.float32)
    for c in range(16):
        for kind, cell in enumerate((c, 240 + c, c * 16, c * 16 + 15)):
            air_rim[kind * 16 + c, cell] = 1
    ocean_rim = np.zeros((160, 256), np.float32)
    side_sel = np.zeros((2, 48, 160), np.float32)
    for j in range(3):
        for c in range(16):
            ocean_rim[j * 16 + c, j * 16 + c] = 1
            ocean_rim[48 + j * 16 + c, (13 + j) * 16 + c] = 1
            for side, (col, start) in enumerate(((13 + j, 128), (j, 96))):
                at = start + (c - 3) * 3 + j
                if c < 3:
                    at = c * 16 + col
                elif c >= 13:
                    at = 48 + (c - 13) * 16 + col
                else:
                    ocean_rim[at, c * 16 + col] = 1
                side_sel[side, j * 16 + c, at] = 1
    strip = np.zeros((4, 256, 128), np.float32)
    for c in range(16):
        for side, cell in enumerate((240 + c, c, c * 16 + 15, c * 16)):
            strip[side, :, side * 16 + c] = join[:, cell]
    up = np.zeros((128, 256), np.float32)
    for r in range(16):
        for q in range(16):
            up[(r // 2) * 8 + q // 2, r * 16 + q] = 1
    pick = np.zeros((4, 256, 256), np.float32)
    for j in range(3):
        for c in range(16):
            cells = ((13 + j) * 16 + c, j * 16 + c, c * 16 + 13 + j, c * 16 + j)
            for side, cell in enumerate(cells):
                pick[side, cell, side * 64 + j * 16 + c] = 1
    up_rim = np.einsum("qc,scd->sqd", up, pick)
    shift = np.zeros((512, 7, 384), np.float32)
    for j in range(7):
        for q in range(16):
            col = q + j
            for r in range(22):
                at = r * 16 + q
                if 3 <= r < 19 and 3 <= col < 19:
                    shift[(r - 3) * 16 + col - 3, j, at] = 1
                elif 3 <= col < 19:
                    side, k = (0, r) if r < 3 else (1, r - 19)
                    shift[256 + side * 64 + k * 16 + col - 3, j, at] = 1
                elif 3 <= r < 19:
                    side, k = (2, col) if col < 3 else (3, col - 19)
                    shift[256 + side * 64 + k * 16 + r - 3, j, at] = 1
    mean = np.zeros((2, 256, 128), np.float32)
    for r in range(16):
        for q in range(16):
            for h in range(2):
                mean[h, r * 16 + q, h * 64 + (r // 2) * 8 + q // 2] = 0.25
    tables = (
        split,
        join,
        air_rim,
        ocean_rim,
        side_sel,
        strip.reshape(1024, 128),
        up,
        up_rim.reshape(512, 256),
        pick.reshape(1024, 256),
        shift.reshape(512, 2688),
        mean,
    )
    return tuple(jnp.asarray(table, BF) for table in tables)


def coordinates():
    a = lax.axis_index("atm")
    o = lax.axis_index("ocn")
    return a, o, lax.div(a, 4), lax.rem(a, 4)


def axis_partner(mm, phase, d):
    a, o, x, z = coordinates()
    if (mm + phase) % 2 == 0:
        place = lax.rem(z + d, 4)
        return (x * 4 + place, o), place
    place = lax.rem(x + d, 4)
    return (place * 4 + z, o), place


def coupling_partner(k):
    a, o, x, z = coordinates()
    return 2 * o + k, lax.div(a, 2)


def is_me(k):
    a, o, x, z = coordinates()
    return jnp.logical_and(lax.div(a, 2) == o, lax.rem(a, 2) == k)


def remote(src, dst, send, recv, target):
    return pltpu.make_async_remote_copy(
        src_ref=src, dst_ref=dst, send_sem=send, recv_sem=recv,
        device_id=target, device_id_type=MESH)


def greet():
    barrier = pltpu.get_barrier_semaphore()
    a, o, x, z = coordinates()

    def signal(target):
        pl.semaphore_signal(barrier, inc=1, device_id=target, device_id_type=MESH)

    for d in (1, 2, 3):
        for mm in range(2):
            signal(axis_partner(mm, 0, d)[0])
    for d in range(1, 8):
        signal((a, lax.rem(o + d, 8)))
    for k in range(2):
        @pl.when(jnp.logical_not(is_me(k)))
        def _():
            signal(coupling_partner(k))


def await_greetings():
    a, o, x, z = coordinates()
    pl.semaphore_wait(pltpu.get_barrier_semaphore(), 15 - jnp.where(lax.div(a, 2) == o, 1, 0))


def rim_exchange(rd, tiles, nbr, air_rim, g1, st, r2, send, recv):
    a, o, x, z = coordinates()

    def first_copy(mm, d):
        here = axis_partner(mm, 0, 0)[1]
        part = g1[rd][mm].at[here]
        return remote(part, part, send.at[rd, 0, mm, d - 1], recv.at[rd, 0, mm, d - 1],
                      axis_partner(mm, 0, d)[0])

    def second_copy(mm, d):
        here = axis_partner(mm, 1, 0)[1]
        return remote(st.at[rd, mm, d - 1], r2[rd][mm].at[here], send.at[rd, 1, mm, d - 1],
                      recv.at[rd, 1, mm, d - 1], axis_partner(mm, 1, d)[0])

    def begin(mm):
        here = axis_partner(mm, 0, 0)[1]

        @pl.loop(0, 4, unroll=4)
        def _(k):
            rims = dot(air_rim[...], tiles[mm, k]).astype(BF).reshape(4, 16, 256)
            g1[rd][mm][here, pl.ds(k * 4, 4)] = rims

    def send_first(mm):
        for d in (1, 3, 2):
            first_copy(mm, d).start()

    def middle():
        for mm in range(2):
            for d in (1, 2, 3):
                first_copy(mm, d).wait_recv()
            for d in (2, 1, 3, 0):
                (dest, _), place = axis_partner(mm, 1, d)

                @pl.loop(0, 16, unroll=4)
                def _(slot):
                    n = nbr[lax.rem(slot, 4), dest * 4 + lax.div(slot, 4)]
                    owner = lax.div(n, 4)
                    from_place = lax.rem(owner, 4) if mm == 0 else lax.div(owner, 4)
                    side = lax.rem(slot, 4)
                    kind = side + 1 - 2 * lax.rem(side, 2)
                    strip = g1[rd][mm][from_place, lax.rem(n, 4) * 4 + kind]
                    if d == 0:
                        r2[rd][mm][place, slot] = strip
                    else:
                        st[rd, mm, d - 1, slot] = strip

                if d > 0:
                    second_copy(mm, d).start()

    def finish():
        for mm in range(2):
            for d in (1, 2, 3):
                second_copy(mm, d).wait_recv()
        for mm in range(2):
            for d in (1, 2, 3):
                first_copy(mm, d).wait_send()
                second_copy(mm, d).wait_send()

    def strip_of(mm, slot):
        n = nbr[lax.rem(slot, 4), a * 4 + lax.div(slot, 4)]
        owner = lax.div(n, 4)
        place = lax.div(owner, 4) if mm == 0 else lax.rem(owner, 4)
        return r2[rd][mm][place, slot]

    return begin, middle, finish, strip_of, send_first


def stage_tile(k, tile, strips, pad, shifted):
    pad[1:17, 8:24, :] = tile.astype(F32).reshape(16, 16, 256)
    pad[0, 8:24, :] = strips[0].astype(F32)
    pad[17, 8:24, :] = strips[1].astype(F32)
    pad[1:17, 7, :] = strips[2].astype(F32)
    pad[1:17, 24, :] = strips[3].astype(F32)
    for j in range(3):
        shifted[j, k] = pad[:, 7 + j : 23 + j, :].astype(BF).reshape(288, 256)


def convolve(shifted, filt, bias):
    total = None
    for offset in range(9):
        i, j = divmod(offset, 3)
        part = dot(shifted[j, :, i * 16 : i * 16 + 256, :].reshape(1024, 256), filt[offset])
        total = part if total is None else total + part
    return gelu(total + bias[...])


def interior(tile, wide, bias, pad, moved, depth):
    pad[:, 8:24, :] = tile
    for j in range(7):
        moved[j] = pad[:, 5 + j : 21 + j, :]
    for g in range(2):
        lanes = slice(g * 128, g * 128 + 128)
        start = jnp.broadcast_to(bias[:, lanes], (8, 128))
        for c in (0, 8):
            total = [start] * 16
            for j in range(7):
                rows = [moved[j, r, c : c + 8, lanes] for r in range(16)]
                weights = [wide[i * 7 + j, :, lanes] for i in range(7)]
                for p in range(16):
                    for i in range(7):
                        if 0 <= p + i - 3 < 16:
                            total[p] = total[p] + rows[p + i - 3] * weights[i]
            for p in range(16):
                depth[p, c : c + 8, lanes] = total[p]


def rim_sums(side, strip, wide, pad):
    pad[:, 8:24, :] = strip
    total = [None] * 3
    for shift in range(7):
        part = pad[:, 5 + shift : 21 + shift, :].reshape(3, 2, 8, 256)
        for place in range(3):
            for k in range(3):
                along = k - place if side in (0, 2) else 6 + k - place
                if not 0 <= along < 7 or (k < place) == (side in (0, 2)) and k != place:
                    continue
                i, j = (along, shift) if side < 2 else (shift, along)
                term = part[k] * wide[i * 7 + j][None]
                total[place] = term if total[place] is None else total[place] + term
    return [value.reshape(16, 256) for value in total]


def kernel(air, marine, sea, filt_a_far, bias_a, filt_b_far, bias_b, flux_t, exchange, wide_in,
           wide_bias, gain, entry_far, entry_bias, leave_far, skin_t, back,
           split, join, air_rim, ocean_rim, side_sel, strip_sel, up, up_rim, pick, shift_far, mean,
           air_nbr, ocean_nbr, quarter, places,
           result, advanced,
           filt_a, filt_b, entry, leave, shift, fetch,
           first, pad_a, shifted, g00, g01, g10, g11, st, r00, r01, r10, r11,
           rims, sea_all, wet32, flux_own, flux_in, skin_in, back_out, back_in,
           wide, weights, pad_o, moved, pad_r, depth, normed_even, normed_odd, fine_flux,
           fluxes, rim_flux, rim_sea, cells, columns, im2col, centre_q, rim_q,
           asend, arecv, bsend, brecv, ssend, srecv, fsend, frecv, ksend, krecv):
    a, o, x, z = coordinates()
    g1 = ((g00, g01), (g10, g11))
    r2 = ((r00, r01), (r10, r11))
    right = (a, lax.rem(o + 2, 8))
    left = (a, lax.rem(o + 6, 8))
    twin = (a, o + 1 - 2 * lax.rem(o, 2))
    before = lax.rem(o + 6, 8)
    after = lax.rem(o + 2, 8)
    across = lax.rem(o + 4, 8)
    lane = lax.broadcasted_iota(jnp.int32, (16, 128), 1)
    share = jnp.full((16, 256), 0.0625, BF)

    def sea_columns(t):
        row = jnp.broadcast_to(sea[pl.ds(t, 1), :].astype(F32), (16, 256)).astype(BF)
        return dot_t(row, share)

    def rim_copy(block, half, target, n):
        part = rims.at[block, pl.ds(half * 8, 8)]
        return remote(part, part, bsend.at[n], brecv.at[n], target)

    def block_copy(block, n):
        return remote(rims.at[block], rims.at[block], bsend.at[n], brecv.at[n], twin)

    own_copies = [rim_copy(o, 0, right, 0), rim_copy(o, 1, left, 1),
                  rim_copy(o, 1, right, 2), rim_copy(o, 0, left, 3)]
    onward_right = rim_copy(before, 0, right, 4)
    onward_left = rim_copy(after, 1, left, 5)
    twin_copies = [block_copy(o, 6), block_copy(before, 7), block_copy(after, 8),
                   rim_copy(across, 0, twin, 9), rim_copy(across, 1, twin, 10)]

    def sea_copy(d):
        return remote(sea_all.at[o], sea_all.at[o], ssend.at[d - 1], srecv.at[d - 1],
                      (a, lax.rem(o + d, 8)))

    def flux_copy(d):
        part = flux_in.at[pl.ds(8 * o, 8)]
        return remote(part, part, fsend.at[d + 1], frecv.at[d + 1], (a, lax.rem(o + d, 8)))

    def skin_copy(d):
        return remote(skin_in.at[o], skin_in.at[o], ksend.at[d + 1], krecv.at[d + 1],
                      (a, lax.rem(o + d, 8)))

    def first_flux(k):
        return remote(flux_own.at[k], flux_in.at[pl.ds(4 * a, 4)], fsend.at[k], frecv.at[lax.rem(a, 2)],
                      coupling_partner(k))

    def last_skin(k):
        return remote(back_out.at[k], back_in.at[lax.rem(a, 2)], ksend.at[k],
                      krecv.at[lax.rem(a, 2)], coupling_partner(k))

    def unless_me(k, act):
        pl.when(jnp.logical_not(is_me(k)))(act)

    greet()
    fetches = [
        pltpu.make_async_copy(far, near, fetch.at[n])
        for n, (far, near) in enumerate((
            (filt_a_far, filt_a), (shift_far, shift), (entry_far, entry), (leave_far, leave),
            (filt_b_far, filt_b)))
    ]
    for copy in fetches:
        copy.start()
    air_first = rim_exchange(0, air, air_nbr, air_rim, g1, st, r2, asend, arecv)
    air_second = rim_exchange(1, first, air_nbr, air_rim, g1, st, r2, asend, arecv)
    air_first[0](0)
    air_first[0](1)
    sea_all[o] = sea[...].astype(F32).astype(BF)

    @pl.loop(0, 16, unroll=4)
    def _(t):
        wet = (ocean_rim[...].astype(F32) * sea[pl.ds(t, 1), :].astype(F32)).astype(BF)
        rims[o, t] = dot(wet, marine[t]).astype(BF)

    await_greetings()
    air_first[4](0)
    air_first[4](1)
    for copy in own_copies:
        copy.start()
    twin_copies[0].start()
    for d in range(1, 8):
        sea_copy(d).start()

    spread_in = exchange[...].astype(F32)
    weights[...] = jnp.zeros(weights.shape, BF)
    for i in range(7):
        for j in range(7):
            row = wide_in[i * 7 + j : i * 7 + j + 1, :].astype(F32)
            wide[i * 7 + j] = jnp.broadcast_to(row, (8, 256))
            at = (i % 2) * 128 + j * 16
            weights[i // 2, at : at + 16, :] = (spread_in * row).astype(BF)
    pad_o[...] = jnp.zeros(pad_o.shape, F32)
    pad_r[...] = jnp.zeros(pad_r.shape, F32)
    pad_a[...] = jnp.zeros(pad_a.shape, F32)

    def interiors(low, high):
        @pl.loop(low, high)
        def _(t):
            tile = (marine[t].astype(F32) * sea_columns(t)).reshape(16, 16, 256)
            interior(tile, wide, wide_bias, pad_o, moved, depth.at[t])

    interiors(0, 5)
    air_first[1]()
    interiors(5, 11)
    air_first[2]()
    fetches[0].wait()

    for mm in range(2):
        @pl.loop(0, 4)
        def _(k):
            strips = [air_first[3](mm, k * 4 + s) for s in range(4)]
            stage_tile(k, air[mm, k], strips, pad_a, shifted)

        first[mm] = (air[mm].astype(F32).reshape(1024, 256)
                     + convolve(shifted, filt_a, bias_a)).astype(BF).reshape(4, 256, 256)

        @pl.loop(0, 4)
        def _(k):
            flux = lax.dot_general(flux_t[...], first[mm, k], (((1,), (1,)), ((), ())),
                                   preferred_element_type=F32).astype(BF)
            quads = dot(flux, split[...])
            low = lax.rem(places[a * 8 + k * 2], 2)
            high = lax.rem(places[a * 8 + k * 2 + 1], 2)
            chosen = jnp.where(lane < 64, low, high)
            flux_own[mm, k] = jnp.where(
                chosen == 1, quads[:, 128:], quads[:, :128]).astype(BF)

        unless_me(mm, lambda: first_flux(mm).start())

        @pl.when(is_me(mm))
        def _():
            flux_in[pl.ds(4 * a, 4)] = flux_own[mm]

        air_second[0](mm)
        air_second[4](mm)

    own_copies[0].wait_recv()
    onward_right.start()
    own_copies[1].wait_recv()
    onward_left.start()

    interiors(11, 14)
    for k in range(2):
        def arrival():
            remote(flux_own.at[0], flux_in.at[pl.ds(8 * o + 4 * k, 4)], fsend.at[k], frecv.at[k],
                   coupling_partner(k)).wait_recv()
        unless_me(k, arrival)
    for d in range(1, 8):
        flux_copy(d).start()
    interiors(14, 16)
    air_second[1]()
    for d in range(1, 8):
        sea_copy(d).wait_recv()
    wet32[...] = sea_all[...].astype(F32).reshape(128, 1, 256)
    for d in range(1, 8):
        flux_copy(d).wait_recv()
    own_copies[2].wait_recv()
    twin_copies[1].start()
    own_copies[3].wait_recv()
    twin_copies[2].start()

    def quadrant(tile):
        q = quarter[tile]
        both = flux_in[lax.div(q, 4)].astype(F32)
        upper = lax.rem(lax.div(q, 2), 2)
        turned = jnp.where(upper == 1, pltpu.roll(both, 64, 1), both)
        return jnp.where(lane < 64, turned, 0.0).astype(BF)

    @pl.loop(0, 16)
    def _(t):
        rows = pl.ds(pl.multiple_of(t * 16, 16), 16)
        fluxes[rows, :] = quadrant(o * 16 + t)
        for s in range(4):
            n = ocean_nbr[s, o * 16 + t]
            rim_flux[rows, s * 128 : (s + 1) * 128] = quadrant(n)
            rim_sea[pl.ds(t, 1), s * 256 : (s + 1) * 256] = wet32[n]

    fine = dot(fluxes[...], up[...])
    sea_here = jnp.broadcast_to(sea[...].astype(F32).reshape(16, 1, 256), (16, 16, 256))
    cells[:, 0:256] = (fine * sea_here.reshape(256, 256)).astype(BF)
    rim_wet = dot(rim_sea[...].astype(BF), pick[...])
    rim_wet = jnp.broadcast_to(rim_wet.reshape(16, 1, 256), (16, 16, 256)).reshape(256, 256)
    cells[:, 256:512] = (dot(rim_flux[...], up_rim[...]) * rim_wet).astype(BF)
    fine_flux[...] = fine.astype(BF)

    fetches[1].wait()
    columns[:, 112:128, :] = jnp.zeros((16, 16, 384), BF)
    for j in range(7):
        shifts = dot(cells[...], shift[:, j * 384 : j * 384 + 384]).astype(BF)
        columns[:, j * 16 : j * 16 + 16, :] = shifts.reshape(16, 16, 384)

    @pl.loop(0, 16)
    def _(t):
        turned = columns[t].astype(F32).T.astype(BF)
        im2col[t, :, 0:128] = turned
        im2col[t, 0:368, 128:256] = turned[16:384]
        im2col[t, 368:384, 128:256] = jnp.zeros((16, 128), BF)

    @pl.loop(0, 4)
    def _(p):
        four = pl.ds(p * 4, 4)
        total = depth[four].reshape(1024, 256)
        for i in range(4):
            total = total + dot(im2col[four, i * 32 : i * 32 + 256, :].reshape(1024, 256),
                                weights[i])
        depth[four] = total.reshape(4, 16, 16, 256)

    onward_right.wait_recv()
    twin_copies[3].start()
    onward_left.wait_recv()
    twin_copies[4].start()
    for copy in twin_copies:
        copy.wait_recv()

    fetches[2].wait()
    fetches[3].wait()
    leave[...] = (leave[...].astype(F32) * 0.5).astype(BF)

    def add_rim(t, h, s):
        n = ocean_nbr[s, o * 16 + t]
        beside = rims[lax.div(n, 16), lax.rem(n, 16)]
        if s < 2:
            strip = beside[48 - 48 * s : 96 - 48 * s].astype(F32)
        else:
            strip = dot(side_sel[s - 2], beside)
        sums = rim_sums(s, strip.reshape(3, 16, 256), wide, pad_r.at[h * 4 + s])
        for place in range(3):
            if s < 2:
                row = place + 13 * s
                depth[t, row] = depth[t, row] + sums[place]
            else:
                col = place + 13 * (s - 2)
                depth[t, :, col, :] = depth[t, :, col, :] + sums[place]

    def norm(t, h, normed):
        value = depth[t].reshape(256, 256)
        value = value - jnp.mean(value, axis=1, keepdims=True)
        spread = jnp.mean(value * value, axis=1, keepdims=True)
        value = value * lax.rsqrt(spread + 1e-6) * gain[...]
        normed[h * 256 : h * 256 + 256] = value.astype(BF)

    def emit(p, outer):
        pair = jnp.zeros((16, 128), F32)
        for h in range(2):
            t = p * 2 + h
            rows = pl.ds(pl.multiple_of(t * 16, 16), 16)
            forced = marine[t].astype(F32) + dot_t(fine_flux[rows, :], exchange[...])
            whole = forced + outer[h * 256 : h * 256 + 256]
            done = (sea_columns(t) * whole).astype(BF)
            advanced[t] = done
            surface = lax.dot_general(skin_t[...], done, (((1,), (1,)), ((), ())),
                                      preferred_element_type=F32).astype(BF)
            pair = pair + dot(surface, mean[h])
        skin_in[o, p] = pair.astype(BF)

    def work(p, now, later):
        outer = None
        for part in range(4):
            if now is not None:
                lanes = slice(part * 256, part * 256 + 256)
                inner = dot(now[...], entry[:, lanes]) + entry_bias[:, lanes]
                inner = (inner + inner * jnp.tanh(inner * (C0 + C1 * (inner * inner)))).astype(BF)
                term = dot(inner, leave[lanes, :])
                outer = term if outer is None else outer + term
            if later is not None:
                for h, s in ((part // 2, part % 2 * 2), (part // 2, part % 2 * 2 + 1)):
                    add_rim(p * 2 + 2 + h, h, s)
        if later is not None:
            for h in range(2):
                norm(p * 2 + 2 + h, h, later)
        if now is not None:
            emit(p, outer)

    even, odd = normed_even, normed_odd
    work(jnp.int32(-1), None, even)

    @pl.loop(0, 3)
    def _(q):
        work(2 * q, even, odd)
        work(2 * q + 1, odd, even)

    work(jnp.int32(6), even, odd)
    work(jnp.int32(7), odd, None)

    for d in range(1, 8):
        skin_copy(d).start()
    air_second[2]()
    for d in range(1, 8):
        skin_copy(d).wait_recv()

    fetches[4].wait()

    def half(j):
        s = lax.div(places[j], 2)
        b = lax.rem(places[j], 2)
        both = skin_in[lax.div(s, 16), lax.div(lax.rem(s, 16), 2)].astype(F32)
        turned = jnp.where(lax.rem(s, 2) == b, both, pltpu.roll(both, 64, 1))
        inside = jnp.where(lane < 64, 0, 1) == b
        return jnp.where(inside, turned, 0.0).astype(BF)

    @pl.loop(0, 8)
    def _(k):
        rows = pl.ds(pl.multiple_of(k * 16, 16), 16)
        tile = o * 8 + k
        for h in range(2):
            centre_q[rows, h * 128 : h * 128 + 128] = half(tile * 2 + h)
            for s in range(4):
                n = air_nbr[s, tile]
                at = s * 256 + h * 128
                rim_q[rows, at : at + 128] = half(n * 2 + h)

    centre = dot(centre_q[...], join[...]).astype(BF)
    rim = dot(rim_q[...], strip_sel[...]).astype(BF)
    for k in range(2):
        back_out[k, :, 0:256] = centre[k * 64 : k * 64 + 64]
        back_out[k, :, 256:384] = rim[k * 64 : k * 64 + 64]
        unless_me(k, lambda: last_skin(k).start())

        @pl.when(is_me(k))
        def _():
            back_in[k] = back_out[k]

    for mm in range(2):
        def arrival():
            remote(back_out.at[0], back_in.at[mm], ksend.at[mm], krecv.at[mm],
                   coupling_partner(mm)).wait_recv()
        unless_me(mm, arrival)

        @pl.loop(0, 4)
        def _(k):
            rows = pl.ds(pl.multiple_of(k * 16, 16), 16)
            add = dot_t(back_in[mm, rows, 0:256], back[...])
            tile = (first[mm, k].astype(F32) + add).astype(BF)
            result[mm, k] = tile
            extra = dot_t(back_in[mm, rows, 256:384], back[...])
            strips = [
                (air_second[3](mm, k * 4 + s).astype(F32) + extra[s * 16 : s * 16 + 16]).astype(BF)
                for s in range(4)
            ]
            stage_tile(k, tile, strips, pad_a, shifted)

        result[mm] = (result[mm].astype(F32).reshape(1024, 256)
                      + convolve(shifted, filt_b, bias_b)).astype(BF).reshape(4, 256, 256)

    for copy in own_copies + [onward_right, onward_left] + twin_copies:
        copy.wait_send()
    for d in range(1, 8):
        sea_copy(d).wait_send()
        flux_copy(d).wait_send()
        skin_copy(d).wait_send()
    for k in range(2):
        unless_me(k, lambda: first_flux(k).wait_send())
        unless_me(k, lambda: last_skin(k).wait_send())


def on_device(
    air_member_values,
    marine_member_values,
    air_neighbour_faces,
    marine_neighbour_faces,
    marine_spanned_quarter,
    water_cell_indicator,
    initial_air_filter,
    initial_filter_offset,
    later_air_filter,
    later_filter_offset,
    air_to_exchange_matrix,
    exchange_to_marine_matrix,
    marine_wide_filter,
    wide_filter_offset,
    marine_rescale_factor,
    hidden_entry_matrix,
    hidden_entry_offset,
    hidden_exit_matrix,
    marine_to_skin_matrix,
    skin_to_air_matrix,
):
    index = lax.broadcasted_iota(jnp.int32, (128, 128), 0)
    tile = lax.broadcasted_iota(jnp.int32, (128, 128), 1)
    covered = jnp.broadcast_to(marine_spanned_quarter[None, :], (128, 128))
    code = jnp.where((covered >> 1) == index, 2 * tile + (covered & 1), 0)
    places = jnp.sum(code, axis=1)
    strips = pltpu.VMEM((4, 16, 16, 256), BF)
    dma = pltpu.SemaphoreType.DMA
    atm_next, advanced = pl.pallas_call(
        kernel,
        out_shape=(
            jax.ShapeDtypeStruct((2, 4, 256, 256), BF),
            jax.ShapeDtypeStruct((16, 256, 256), BF),
        ),
        in_specs=[VMEM] * 3 + [HBM, VMEM, HBM] + [VMEM] * 6 + [HBM, VMEM, HBM] + [VMEM] * 11
        + [HBM, VMEM] + [SMEM] * 4,
        out_specs=(VMEM, VMEM),
        scratch_shapes=[
            pltpu.VMEM((9, 256, 256), BF),
            pltpu.VMEM((9, 256, 256), BF),
            pltpu.VMEM((256, 1024), BF),
            pltpu.VMEM((1024, 256), BF),
            pltpu.VMEM((512, 2688), BF),
            dma((5,)),
            pltpu.VMEM((2, 4, 256, 256), BF),
            pltpu.VMEM((18, 32, 256), F32),
            pltpu.VMEM((3, 4, 288, 256), BF),
            strips, strips, strips, strips,
            pltpu.VMEM((2, 2, 3, 16, 16, 256), BF),
            strips, strips, strips, strips,
            pltpu.VMEM((8, 16, 160, 256), BF),
            pltpu.VMEM((8, 16, 256), BF),
            pltpu.VMEM((128, 1, 256), F32),
            pltpu.VMEM((2, 4, 16, 128), BF),
            pltpu.VMEM((64, 16, 128), BF),
            pltpu.VMEM((8, 8, 16, 128), BF),
            pltpu.VMEM((2, 64, 384), BF),
            pltpu.VMEM((2, 64, 384), BF),
            pltpu.VMEM((49, 8, 256), F32),
            pltpu.VMEM((4, 256, 256), BF),
            pltpu.VMEM((16, 32, 256), F32),
            pltpu.VMEM((7, 16, 16, 256), F32),
            pltpu.VMEM((8, 3, 32, 256), F32),
            pltpu.VMEM((16, 16, 16, 256), F32),
            pltpu.VMEM((512, 256), BF),
            pltpu.VMEM((512, 256), BF),
            pltpu.VMEM((256, 256), BF),
            pltpu.VMEM((256, 128), BF),
            pltpu.VMEM((256, 512), BF),
            pltpu.VMEM((16, 1024), F32),
            pltpu.VMEM((256, 512), BF),
            pltpu.VMEM((16, 128, 384), BF),
            pltpu.VMEM((16, 384, 256), BF),
            pltpu.VMEM((128, 256), BF),
            pltpu.VMEM((128, 1024), BF),
            dma((2, 2, 2, 3)), dma((2, 2, 2, 3)),
            dma((11,)), dma((11,)),
            dma((7,)), dma((7,)),
            dma((9,)), dma((9,)),
            dma((9,)), dma((9,)),
        ],
        compiler_params=pltpu.CompilerParams(
            collective_id=0, has_side_effects=True, vmem_limit_bytes=60 * 1024 * 1024),
    )(
        air_member_values, marine_member_values.reshape(16, 256, 256), water_cell_indicator,
        initial_air_filter, initial_filter_offset.reshape(1, 256),
        later_air_filter, later_filter_offset.reshape(1, 256),
        air_to_exchange_matrix.T, exchange_to_marine_matrix, marine_wide_filter,
        wide_filter_offset.reshape(1, 256), marine_rescale_factor.reshape(1, 256),
        hidden_entry_matrix, hidden_entry_offset.reshape(1, 1024), hidden_exit_matrix,
        marine_to_skin_matrix.T, skin_to_air_matrix, *cell_tables(),
        air_neighbour_faces.T, marine_neighbour_faces.T, marine_spanned_quarter, places,
    )
    return atm_next, advanced.reshape(1, 16, 256, 256)


def solution(mesh):
    in_specs = (
        P("ocn", "atm", None, None),
        P("atm", "ocn", None, None),
        P(),
        P(),
        P(),
        P("ocn", None),
    ) + (P(),) * 14
    out_specs = (P("ocn", "atm", None, None), P("atm", "ocn", None, None))
    return jax.shard_map(
        on_device, mesh=mesh, in_specs=in_specs, out_specs=out_specs, check_vma=False
    )
```

```python
import jax
import jax.numpy as jnp
import numpy as np
from jax import lax
from jax.experimental import pallas as pl
from jax.experimental.pallas import tpu as pltpu
from jax.sharding import PartitionSpec as P

BF = jnp.bfloat16
F32 = jnp.float32
MESH = pl.DeviceIdType.MESH
VMEM = pl.BlockSpec(memory_space=pltpu.VMEM)
SMEM = pl.BlockSpec(memory_space=pltpu.SMEM)
HBM = pl.BlockSpec(memory_space=pl.ANY)
C0 = 0.7978845608028654
C1 = C0 * 0.044715


def gelu(x):
    half = 0.5 * x
    return half + half * jnp.tanh(x * (C0 + C1 * (x * x)))


def dot(a, b):
    return jnp.dot(a, b, preferred_element_type=F32)


def dot_t(a, b):
    return lax.dot_general(a, b, (((0,), (0,)), ((), ())), preferred_element_type=F32)


def cell_tables():
    split = np.zeros((256, 256), np.float32)
    join = np.zeros((256, 256), np.float32)
    for r in range(16):
        for q in range(16):
            a, b = r // 8, q // 8
            cell = (r % 8) * 8 + q % 8
            split[r * 16 + q, b * 128 + a * 64 + cell] = 1
            join[a * 128 + b * 64 + cell, r * 16 + q] = 1
    air_rim = np.zeros((64, 256), np.float32)
    for c in range(16):
        for kind, cell in enumerate((c, 240 + c, c * 16, c * 16 + 15)):
            air_rim[kind * 16 + c, cell] = 1
    ocean_rim = np.zeros((160, 256), np.float32)
    side_sel = np.zeros((2, 48, 160), np.float32)
    for j in range(3):
        for c in range(16):
            ocean_rim[j * 16 + c, j * 16 + c] = 1
            ocean_rim[48 + j * 16 + c, (13 + j) * 16 + c] = 1
            for side, (col, start) in enumerate(((13 + j, 128), (j, 96))):
                at = start + (c - 3) * 3 + j
                if c < 3:
                    at = c * 16 + col
                elif c >= 13:
                    at = 48 + (c - 13) * 16 + col
                else:
                    ocean_rim[at, c * 16 + col] = 1
                side_sel[side, j * 16 + c, at] = 1
    strip = np.zeros((4, 256, 128), np.float32)
    for c in range(16):
        for side, cell in enumerate((240 + c, c, c * 16 + 15, c * 16)):
            strip[side, :, side * 16 + c] = join[:, cell]
    up = np.zeros((128, 256), np.float32)
    for r in range(16):
        for q in range(16):
            up[(r // 2) * 8 + q // 2, r * 16 + q] = 1
    pick = np.zeros((4, 256, 256), np.float32)
    for j in range(3):
        for c in range(16):
            cells = ((13 + j) * 16 + c, j * 16 + c, c * 16 + 13 + j, c * 16 + j)
            for side, cell in enumerate(cells):
                pick[side, cell, side * 64 + j * 16 + c] = 1
    up_rim = np.einsum("qc,scd->sqd", up, pick)
    shift = np.zeros((512, 7, 384), np.float32)
    for j in range(7):
        for q in range(16):
            col = q + j
            for r in range(22):
                at = r * 16 + q
                if 3 <= r < 19 and 3 <= col < 19:
                    shift[(r - 3) * 16 + col - 3, j, at] = 1
                elif 3 <= col < 19:
                    side, k = (0, r) if r < 3 else (1, r - 19)
                    shift[256 + side * 64 + k * 16 + col - 3, j, at] = 1
                elif 3 <= r < 19:
                    side, k = (2, col) if col < 3 else (3, col - 19)
                    shift[256 + side * 64 + k * 16 + r - 3, j, at] = 1
    shift_air = np.zeros((384, 3, 384), np.float32)
    for j in range(3):
        for q in range(16):
            col = q + j
            for r in range(18):
                at = r * 16 + q
                if 1 <= r < 17 and 1 <= col < 17:
                    shift_air[(r - 1) * 16 + col - 1, j, at] = 1
                elif 1 <= col < 17:
                    shift_air[256 + (0 if r < 1 else 16) + col - 1, j, at] = 1
                elif 1 <= r < 17:
                    shift_air[256 + (32 if col < 1 else 48) + r - 1, j, at] = 1
    mean = np.zeros((2, 256, 128), np.float32)
    for r in range(16):
        for q in range(16):
            for h in range(2):
                mean[h, r * 16 + q, h * 64 + (r // 2) * 8 + q // 2] = 0.25
    tables = (
        split,
        join,
        air_rim,
        ocean_rim,
        side_sel,
        strip.reshape(1024, 128),
        up,
        up_rim.reshape(512, 256),
        pick.reshape(1024, 256),
        shift.reshape(512, 2688),
        shift_air.reshape(384, 1152),
        mean,
    )
    return tuple(jnp.asarray(table, BF) for table in tables)


def coordinates():
    a = lax.axis_index("atm")
    o = lax.axis_index("ocn")
    return a, o, lax.div(a, 4), lax.rem(a, 4)


def axis_partner(mm, phase, d):
    a, o, x, z = coordinates()
    if (mm + phase) % 2 == 0:
        place = lax.rem(z + d, 4)
        return (x * 4 + place, o), place
    place = lax.rem(x + d, 4)
    return (place * 4 + z, o), place


def coupling_partner(k):
    a, o, x, z = coordinates()
    return 2 * o + k, lax.div(a, 2)


def is_me(k):
    a, o, x, z = coordinates()
    return jnp.logical_and(lax.div(a, 2) == o, lax.rem(a, 2) == k)


def remote(src, dst, send, recv, target):
    return pltpu.make_async_remote_copy(
        src_ref=src, dst_ref=dst, send_sem=send, recv_sem=recv,
        device_id=target, device_id_type=MESH)


def greet():
    barrier = pltpu.get_barrier_semaphore()
    a, o, x, z = coordinates()

    def signal(target):
        pl.semaphore_signal(barrier, inc=1, device_id=target, device_id_type=MESH)

    for d in (1, 2, 3):
        for mm in range(2):
            signal(axis_partner(mm, 0, d)[0])
    for d in range(1, 8):
        signal((a, lax.rem(o + d, 8)))
    for k in range(2):
        @pl.when(jnp.logical_not(is_me(k)))
        def _():
            signal(coupling_partner(k))


def await_greetings():
    a, o, x, z = coordinates()
    pl.semaphore_wait(pltpu.get_barrier_semaphore(), 15 - jnp.where(lax.div(a, 2) == o, 1, 0))


def rim_exchange(rd, tiles, nbr, air_rim, g1, st, r2, send, recv):
    a, o, x, z = coordinates()

    def first_copy(mm, d):
        here = axis_partner(mm, 0, 0)[1]
        part = g1[rd][mm].at[here]
        return remote(part, part, send.at[rd, 0, mm, d - 1], recv.at[rd, 0, mm, d - 1],
                      axis_partner(mm, 0, d)[0])

    def second_copy(mm, d):
        here = axis_partner(mm, 1, 0)[1]
        return remote(st.at[rd, mm, d - 1], r2[rd][mm].at[here], send.at[rd, 1, mm, d - 1],
                      recv.at[rd, 1, mm, d - 1], axis_partner(mm, 1, d)[0])

    def begin(mm):
        here = axis_partner(mm, 0, 0)[1]

        @pl.loop(0, 4, unroll=4)
        def _(k):
            rims = dot(air_rim[...], tiles[mm, k]).astype(BF).reshape(4, 16, 256)
            g1[rd][mm][here, pl.ds(k * 4, 4)] = rims

    def send_first(mm):
        for d in (1, 3, 2):
            first_copy(mm, d).start()

    def middle():
        for mm in range(2):
            for d in (1, 2, 3):
                first_copy(mm, d).wait_recv()
            for d in (2, 1, 3, 0):
                (dest, _), place = axis_partner(mm, 1, d)

                @pl.loop(0, 16, unroll=4)
                def _(slot):
                    n = nbr[lax.rem(slot, 4), dest * 4 + lax.div(slot, 4)]
                    owner = lax.div(n, 4)
                    from_place = lax.rem(owner, 4) if mm == 0 else lax.div(owner, 4)
                    side = lax.rem(slot, 4)
                    kind = side + 1 - 2 * lax.rem(side, 2)
                    strip = g1[rd][mm][from_place, lax.rem(n, 4) * 4 + kind]
                    if d == 0:
                        r2[rd][mm][place, slot] = strip
                    else:
                        st[rd, mm, d - 1, slot] = strip

                if d > 0:
                    second_copy(mm, d).start()

    def finish():
        for mm in range(2):
            for d in (1, 2, 3):
                second_copy(mm, d).wait_recv()
        for mm in range(2):
            for d in (1, 2, 3):
                first_copy(mm, d).wait_send()
                second_copy(mm, d).wait_send()

    def strip_of(mm, slot):
        n = nbr[lax.rem(slot, 4), a * 4 + lax.div(slot, 4)]
        owner = lax.div(n, 4)
        place = lax.div(owner, 4) if mm == 0 else lax.rem(owner, 4)
        return r2[rd][mm][place, slot]

    return begin, middle, finish, strip_of, send_first


def stage_tile(k, tile, strips, pad, shifted):
    pad[1:17, 8:24, :] = tile.astype(F32).reshape(16, 16, 256)
    pad[0, 8:24, :] = strips[0].astype(F32)
    pad[17, 8:24, :] = strips[1].astype(F32)
    pad[1:17, 7, :] = strips[2].astype(F32)
    pad[1:17, 24, :] = strips[3].astype(F32)
    for j in range(3):
        shifted[j, k] = pad[:, 7 + j : 23 + j, :].astype(BF).reshape(288, 256)


def convolve(shifted, filt):
    total = None
    for offset in range(9):
        i, j = divmod(offset, 3)
        part = dot(shifted[j, :, i * 16 : i * 16 + 256, :].reshape(1024, 256), filt[offset])
        total = part if total is None else total + part
    return total


def interior(tile, wide, bias, pad, moved, depth):
    pad[:, 8:24, :] = tile
    for j in range(7):
        moved[j] = pad[:, 5 + j : 21 + j, :]
    for g in range(2):
        lanes = slice(g * 128, g * 128 + 128)
        start = jnp.broadcast_to(bias[:, lanes], (8, 128))
        for c in (0, 8):
            total = [start] * 16
            for j in range(7):
                rows = [moved[j, r, c : c + 8, lanes] for r in range(16)]
                weights = [wide[i * 7 + j, :, lanes] for i in range(7)]
                for p in range(16):
                    for i in range(7):
                        if 0 <= p + i - 3 < 16:
                            total[p] = total[p] + rows[p + i - 3] * weights[i]
            for p in range(16):
                depth[p, c : c + 8, lanes] = total[p]


def rim_sums(side, strip, wide, pad):
    pad[:, 8:24, :] = strip
    total = [None] * 3
    for shift in range(7):
        part = pad[:, 5 + shift : 21 + shift, :].reshape(3, 2, 8, 256)
        for place in range(3):
            for k in range(3):
                along = k - place if side in (0, 2) else 6 + k - place
                if not 0 <= along < 7 or (k < place) == (side in (0, 2)) and k != place:
                    continue
                i, j = (along, shift) if side < 2 else (shift, along)
                term = part[k] * wide[i * 7 + j][None]
                total[place] = term if total[place] is None else total[place] + term
    return [value.reshape(16, 256) for value in total]


def kernel(air, marine, sea, filt_a_far, bias_a, filt_b_far, bias_b, flux_t, exchange, wide_in,
           wide_bias, gain, entry_far, entry_bias, leave_far, skin_t, back,
           split, join, air_rim, ocean_rim, side_sel, strip_sel, up, up_rim, pick, shift_far, shift_air, mean,
           air_nbr, ocean_nbr, quarter, places,
           result, advanced,
           filt_a, filt_b, entry, leave, shift, fetch,
           first, pad_a, shifted, g00, g01, g10, g11, st, r00, r01, r10, r11,
           rims, sea_all, wet32, flux_own, flux_in, skin_in, back_out, back_in,
           wide, weights, pad_o, moved, pad_r, depth, normed_even, normed_odd, fine_flux,
           fluxes, rim_flux, rim_sea, cells, columns, im2col, centre_q, rim_q,
           sums, field_weights, field_columns, field_cells,
           asend, arecv, bsend, brecv, ssend, srecv, fsend, frecv, ksend, krecv):
    a, o, x, z = coordinates()
    g1 = ((g00, g01), (g10, g11))
    r2 = ((r00, r01), (r10, r11))
    right = (a, lax.rem(o + 2, 8))
    left = (a, lax.rem(o + 6, 8))
    twin = (a, o + 1 - 2 * lax.rem(o, 2))
    before = lax.rem(o + 6, 8)
    after = lax.rem(o + 2, 8)
    across = lax.rem(o + 4, 8)
    lane = lax.broadcasted_iota(jnp.int32, (16, 128), 1)
    share = jnp.full((16, 256), 0.0625, BF)

    def sea_columns(t):
        row = jnp.broadcast_to(sea[pl.ds(t, 1), :].astype(F32), (16, 256)).astype(BF)
        return dot_t(row, share)

    def rim_copy(block, half, target, n):
        part = rims.at[block, pl.ds(half * 8, 8)]
        return remote(part, part, bsend.at[n], brecv.at[n], target)

    def block_copy(block, n):
        return remote(rims.at[block], rims.at[block], bsend.at[n], brecv.at[n], twin)

    own_copies = [rim_copy(o, 0, right, 0), rim_copy(o, 1, left, 1),
                  rim_copy(o, 1, right, 2), rim_copy(o, 0, left, 3)]
    onward_right = rim_copy(before, 0, right, 4)
    onward_left = rim_copy(after, 1, left, 5)
    twin_copies = [block_copy(o, 6), block_copy(before, 7), block_copy(after, 8),
                   rim_copy(across, 0, twin, 9), rim_copy(across, 1, twin, 10)]

    def sea_copy(d):
        return remote(sea_all.at[o], sea_all.at[o], ssend.at[d - 1], srecv.at[d - 1],
                      (a, lax.rem(o + d, 8)))

    def flux_copy(d):
        part = flux_in.at[pl.ds(8 * o, 8)]
        return remote(part, part, fsend.at[d + 1], frecv.at[d + 1], (a, lax.rem(o + d, 8)))

    def skin_copy(d, half):
        part = skin_in.at[o, pl.ds(half * 4, 4)]
        n = d + 1 + 7 * half
        return remote(part, part, ksend.at[n], krecv.at[n], (a, lax.rem(o + d, 8)))

    def first_flux(k):
        return remote(flux_own.at[k], flux_in.at[pl.ds(4 * a, 4)], fsend.at[k], frecv.at[lax.rem(a, 2)],
                      coupling_partner(k))

    def last_skin(k):
        return remote(back_out.at[k], back_in.at[lax.rem(a, 2)], ksend.at[k],
                      krecv.at[lax.rem(a, 2)], coupling_partner(k))

    def unless_me(k, act):
        pl.when(jnp.logical_not(is_me(k)))(act)

    greet()
    fetches = [
        pltpu.make_async_copy(far, near, fetch.at[n])
        for n, (far, near) in enumerate((
            (filt_a_far, filt_a), (shift_far, shift), (entry_far, entry), (leave_far, leave),
            (filt_b_far, filt_b)))
    ]
    for copy in fetches:
        copy.start()
    air_first = rim_exchange(0, air, air_nbr, air_rim, g1, st, r2, asend, arecv)
    air_second = rim_exchange(1, first, air_nbr, air_rim, g1, st, r2, asend, arecv)
    air_first[0](0)
    air_first[0](1)
    sea_all[o] = sea[...].astype(F32).astype(BF)

    @pl.loop(0, 16, unroll=4)
    def _(t):
        wet = (ocean_rim[...].astype(F32) * sea[pl.ds(t, 1), :].astype(F32)).astype(BF)
        rims[o, t] = dot(wet, marine[t]).astype(BF)

    await_greetings()
    air_first[4](0)
    air_first[4](1)
    for copy in own_copies:
        copy.start()
    twin_copies[0].start()
    for d in range(1, 8):
        sea_copy(d).start()

    spread_in = exchange[...].astype(F32)
    weights[...] = jnp.zeros(weights.shape, BF)
    for i in range(7):
        for j in range(7):
            row = wide_in[i * 7 + j : i * 7 + j + 1, :].astype(F32)
            wide[i * 7 + j] = jnp.broadcast_to(row, (8, 256))
            at = (i % 2) * 128 + j * 16
            weights[i // 2, at : at + 16, :] = (spread_in * row).astype(BF)
    pad_o[...] = jnp.zeros(pad_o.shape, F32)
    pad_r[...] = jnp.zeros(pad_r.shape, F32)
    pad_a[...] = jnp.zeros(pad_a.shape, F32)

    def interiors(low, high):
        @pl.loop(low, high)
        def _(t):
            tile = (marine[t].astype(F32) * sea_columns(t)).reshape(16, 16, 256)
            interior(tile, wide, wide_bias, pad_o, moved, depth.at[t])

    interiors(0, 5)
    air_first[1]()
    interiors(5, 11)
    air_first[2]()
    fetches[0].wait()

    for mm in range(2):
        @pl.loop(0, 4)
        def _(k):
            strips = [air_first[3](mm, k * 4 + s) for s in range(4)]
            stage_tile(k, air[mm, k], strips, pad_a, shifted)

        first[mm] = (air[mm].astype(F32).reshape(1024, 256)
                     + gelu(convolve(shifted, filt_a) + bias_a[...])).astype(BF).reshape(4, 256, 256)

        @pl.loop(0, 4)
        def _(k):
            flux = lax.dot_general(flux_t[...], first[mm, k], (((1,), (1,)), ((), ())),
                                   preferred_element_type=F32).astype(BF)
            quads = dot(flux, split[...])
            low = lax.rem(places[a * 8 + k * 2], 2)
            high = lax.rem(places[a * 8 + k * 2 + 1], 2)
            chosen = jnp.where(lane < 64, low, high)
            flux_own[mm, k] = jnp.where(
                chosen == 1, quads[:, 128:], quads[:, :128]).astype(BF)

        unless_me(mm, lambda: first_flux(mm).start())

        @pl.when(is_me(mm))
        def _():
            flux_in[pl.ds(4 * a, 4)] = flux_own[mm]

        air_second[0](mm)
        air_second[4](mm)

    interiors(11, 14)
    for k in range(2):
        def arrival():
            remote(flux_own.at[0], flux_in.at[pl.ds(8 * o + 4 * k, 4)], fsend.at[k], frecv.at[k],
                   coupling_partner(k)).wait_recv()
        unless_me(k, arrival)
    for d in range(1, 8):
        flux_copy(d).start()
    own_copies[0].wait_recv()
    onward_right.start()
    own_copies[1].wait_recv()
    onward_left.start()
    interiors(14, 16)
    air_second[1]()
    for d in range(1, 8):
        sea_copy(d).wait_recv()
    wet32[...] = sea_all[...].astype(F32).reshape(128, 1, 256)
    for d in range(1, 8):
        flux_copy(d).wait_recv()
    own_copies[2].wait_recv()
    twin_copies[1].start()
    own_copies[3].wait_recv()
    twin_copies[2].start()

    def quadrant(tile):
        q = quarter[tile]
        both = flux_in[lax.div(q, 4)].astype(F32)
        upper = lax.rem(lax.div(q, 2), 2)
        turned = jnp.where(upper == 1, pltpu.roll(both, 64, 1), both)
        return jnp.where(lane < 64, turned, 0.0).astype(BF)

    @pl.loop(0, 16)
    def _(t):
        rows = pl.ds(pl.multiple_of(t * 16, 16), 16)
        fluxes[rows, :] = quadrant(o * 16 + t)
        for s in range(4):
            n = ocean_nbr[s, o * 16 + t]
            rim_flux[rows, s * 128 : (s + 1) * 128] = quadrant(n)
            rim_sea[pl.ds(t, 1), s * 256 : (s + 1) * 256] = wet32[n]

    fine = dot(fluxes[...], up[...])
    sea_here = jnp.broadcast_to(sea[...].astype(F32).reshape(16, 1, 256), (16, 16, 256))
    cells[:, 0:256] = (fine * sea_here.reshape(256, 256)).astype(BF)
    rim_wet = dot(rim_sea[...].astype(BF), pick[...])
    rim_wet = jnp.broadcast_to(rim_wet.reshape(16, 1, 256), (16, 16, 256)).reshape(256, 256)
    cells[:, 256:512] = (dot(rim_flux[...], up_rim[...]) * rim_wet).astype(BF)
    fine_flux[...] = fine.astype(BF)

    fetches[1].wait()
    columns[:, 112:128, :] = jnp.zeros((16, 16, 384), BF)
    for j in range(7):
        shifts = dot(cells[...], shift[:, j * 384 : j * 384 + 384]).astype(BF)
        columns[:, j * 16 : j * 16 + 16, :] = shifts.reshape(16, 16, 384)

    @pl.loop(0, 16)
    def _(t):
        turned = columns[t].astype(F32).T.astype(BF)
        im2col[t, :, 0:128] = turned
        im2col[t, 0:368, 128:256] = turned[16:384]
        im2col[t, 368:384, 128:256] = jnp.zeros((16, 128), BF)

    @pl.loop(0, 4)
    def _(p):
        four = pl.ds(p * 4, 4)
        total = depth[four].reshape(1024, 256)
        for i in range(4):
            total = total + dot(im2col[four, i * 32 : i * 32 + 256, :].reshape(1024, 256),
                                weights[i])
        depth[four] = total.reshape(4, 16, 16, 256)

    def early_sums(mm):
        @pl.loop(0, 4)
        def _(k):
            strips = [air_second[3](mm, k * 4 + s) for s in range(4)]
            stage_tile(k, first[mm, k], strips, pad_a, shifted)

        sums[mm] = convolve(shifted, filt_b)

    air_second[2]()
    fetches[4].wait()
    early_sums(0)

    onward_right.wait_recv()
    twin_copies[3].start()
    onward_left.wait_recv()
    twin_copies[4].start()
    field_weights[...] = jnp.zeros(field_weights.shape, BF)
    for h in range(2):
        for i in range(3):
            for j in range(3):
                at = h * 64 + j * 16
                field_weights[h, i, at : at + 16] = dot(back[...], filt_b[3 * i + j]).astype(BF)
    field_columns[...] = jnp.zeros(field_columns.shape, BF)
    for copy in twin_copies:
        copy.wait_recv()

    fetches[2].wait()
    fetches[3].wait()
    leave[...] = (leave[...].astype(F32) * 0.5).astype(BF)

    def add_rim(t, h, s):
        n = ocean_nbr[s, o * 16 + t]
        beside = rims[lax.div(n, 16), lax.rem(n, 16)]
        if s < 2:
            strip = beside[48 - 48 * s : 96 - 48 * s].astype(F32)
        else:
            strip = dot(side_sel[s - 2], beside)
        sums = rim_sums(s, strip.reshape(3, 16, 256), wide, pad_r.at[h * 4 + s])
        for place in range(3):
            if s < 2:
                row = place + 13 * s
                depth[t, row] = depth[t, row] + sums[place]
            else:
                col = place + 13 * (s - 2)
                depth[t, :, col, :] = depth[t, :, col, :] + sums[place]

    def norm(t, h, normed):
        value = depth[t].reshape(256, 256)
        value = value - jnp.mean(value, axis=1, keepdims=True)
        spread = jnp.mean(value * value, axis=1, keepdims=True)
        value = value * lax.rsqrt(spread + 1e-6) * gain[...]
        normed[h * 256 : h * 256 + 256] = value.astype(BF)

    def emit(p, outer):
        pair = jnp.zeros((16, 128), F32)
        for h in range(2):
            t = p * 2 + h
            rows = pl.ds(pl.multiple_of(t * 16, 16), 16)
            forced = marine[t].astype(F32) + dot_t(fine_flux[rows, :], exchange[...])
            whole = forced + outer[h * 256 : h * 256 + 256]
            done = (sea_columns(t) * whole).astype(BF)
            advanced[t] = done
            surface = lax.dot_general(skin_t[...], done, (((1,), (1,)), ((), ())),
                                      preferred_element_type=F32).astype(BF)
            pair = pair + dot(surface, mean[h])
        skin_in[o, p] = pair.astype(BF)

    def work(p, now, later):
        outer = None
        for part in range(4):
            if now is not None:
                lanes = slice(part * 256, part * 256 + 256)
                inner = dot(now[...], entry[:, lanes]) + entry_bias[:, lanes]
                inner = (inner + inner * jnp.tanh(inner * (C0 + C1 * (inner * inner)))).astype(BF)
                term = dot(inner, leave[lanes, :])
                outer = term if outer is None else outer + term
            if later is not None:
                for h, s in ((part // 2, part % 2 * 2), (part // 2, part % 2 * 2 + 1)):
                    add_rim(p * 2 + 2 + h, h, s)
        if later is not None:
            for h in range(2):
                norm(p * 2 + 2 + h, h, later)
        if now is not None:
            emit(p, outer)

    even, odd = normed_even, normed_odd
    work(jnp.int32(-1), None, even)

    @pl.loop(0, 3)
    def _(q):
        work(2 * q, even, odd)
        work(2 * q + 1, odd, even)

    for d in range(1, 8):
        skin_copy(d, 0).start()
    work(jnp.int32(6), even, odd)
    work(jnp.int32(7), odd, None)

    for d in range(1, 8):
        skin_copy(d, 1).start()
    early_sums(1)

    for d in range(1, 8):
        skin_copy(d, 0).wait_recv()
        skin_copy(d, 1).wait_recv()

    def half(j):
        s = lax.div(places[j], 2)
        b = lax.rem(places[j], 2)
        both = skin_in[lax.div(s, 16), lax.div(lax.rem(s, 16), 2)].astype(F32)
        turned = jnp.where(lax.rem(s, 2) == b, both, pltpu.roll(both, 64, 1))
        inside = jnp.where(lane < 64, 0, 1) == b
        return jnp.where(inside, turned, 0.0).astype(BF)

    @pl.loop(0, 8)
    def _(k):
        rows = pl.ds(pl.multiple_of(k * 16, 16), 16)
        tile = o * 8 + k
        for h in range(2):
            centre_q[rows, h * 128 : h * 128 + 128] = half(tile * 2 + h)
            for s in range(4):
                n = air_nbr[s, tile]
                at = s * 256 + h * 128
                rim_q[rows, at : at + 128] = half(n * 2 + h)

    centre = dot(centre_q[...], join[...]).astype(BF)
    rim = dot(rim_q[...], strip_sel[...]).astype(BF)
    for k in range(2):
        back_out[k, :, 0:256] = centre[k * 64 : k * 64 + 64]
        back_out[k, :, 256:384] = rim[k * 64 : k * 64 + 64]
        unless_me(k, lambda: last_skin(k).start())

        @pl.when(is_me(k))
        def _():
            back_in[k] = back_out[k]

    for mm in range(2):
        def arrival():
            remote(back_out.at[0], back_in.at[mm], ksend.at[mm], krecv.at[mm],
                   coupling_partner(mm)).wait_recv()
        unless_me(mm, arrival)

    for j in range(3):
        moved_fields = dot(back_in[...].reshape(128, 384), shift_air[:, j * 384 : j * 384 + 384])
        moved_fields = moved_fields.astype(BF).reshape(4, 2, 16, 384)
        for h in range(2):
            at = h * 64 + j * 16
            field_columns[:, at : at + 16, :] = moved_fields[:, h]
    for p in range(4):
        field_cells[p] = field_columns[p].astype(F32).T.astype(BF)
    for mm in range(2):
        parts = []
        for h in range(2):
            total = None
            for i in range(3):
                rows = field_cells[2 * mm : 2 * mm + 2, i * 16 : i * 16 + 256, :]
                term = dot(rows.reshape(512, 128), field_weights[h, i])
                total = term if total is None else total + term
            parts.append(total.reshape(2, 256, 256))
        for k in range(4):
            rows = slice(k * 16, k * 16 + 16)
            add = dot_t(back_in[mm, rows, 0:256], back[...])
            tile = (first[mm, k].astype(F32) + add).astype(BF).astype(F32)
            total = sums[mm, k * 256 : k * 256 + 256] + parts[k % 2][k // 2] + bias_b[...]
            result[mm, k] = (tile + gelu(total)).astype(BF)

    for copy in own_copies + [onward_right, onward_left] + twin_copies:
        copy.wait_send()
    for d in range(1, 8):
        sea_copy(d).wait_send()
        flux_copy(d).wait_send()
        skin_copy(d, 0).wait_send()
        skin_copy(d, 1).wait_send()
    for k in range(2):
        unless_me(k, lambda: first_flux(k).wait_send())
        unless_me(k, lambda: last_skin(k).wait_send())


def on_device(
    air_member_values,
    marine_member_values,
    air_neighbour_faces,
    marine_neighbour_faces,
    marine_spanned_quarter,
    water_cell_indicator,
    initial_air_filter,
    initial_filter_offset,
    later_air_filter,
    later_filter_offset,
    air_to_exchange_matrix,
    exchange_to_marine_matrix,
    marine_wide_filter,
    wide_filter_offset,
    marine_rescale_factor,
    hidden_entry_matrix,
    hidden_entry_offset,
    hidden_exit_matrix,
    marine_to_skin_matrix,
    skin_to_air_matrix,
):
    index = lax.broadcasted_iota(jnp.int32, (128, 128), 0)
    tile = lax.broadcasted_iota(jnp.int32, (128, 128), 1)
    covered = jnp.broadcast_to(marine_spanned_quarter[None, :], (128, 128))
    code = jnp.where((covered >> 1) == index, 2 * tile + (covered & 1), 0)
    places = jnp.sum(code, axis=1)
    strips = pltpu.VMEM((4, 16, 16, 256), BF)
    dma = pltpu.SemaphoreType.DMA
    atm_next, advanced = pl.pallas_call(
        kernel,
        out_shape=(
            jax.ShapeDtypeStruct((2, 4, 256, 256), BF),
            jax.ShapeDtypeStruct((16, 256, 256), BF),
        ),
        in_specs=[VMEM] * 3 + [HBM, VMEM, HBM] + [VMEM] * 6 + [HBM, VMEM, HBM] + [VMEM] * 11
        + [HBM, VMEM, VMEM] + [SMEM] * 4,
        out_specs=(VMEM, VMEM),
        scratch_shapes=[
            pltpu.VMEM((9, 256, 256), BF),
            pltpu.VMEM((9, 256, 256), BF),
            pltpu.VMEM((256, 1024), BF),
            pltpu.VMEM((1024, 256), BF),
            pltpu.VMEM((512, 2688), BF),
            dma((5,)),
            pltpu.VMEM((2, 4, 256, 256), BF),
            pltpu.VMEM((18, 32, 256), F32),
            pltpu.VMEM((3, 4, 288, 256), BF),
            strips, strips, strips, strips,
            pltpu.VMEM((2, 2, 3, 16, 16, 256), BF),
            strips, strips, strips, strips,
            pltpu.VMEM((8, 16, 160, 256), BF),
            pltpu.VMEM((8, 16, 256), BF),
            pltpu.VMEM((128, 1, 256), F32),
            pltpu.VMEM((2, 4, 16, 128), BF),
            pltpu.VMEM((64, 16, 128), BF),
            pltpu.VMEM((8, 8, 16, 128), BF),
            pltpu.VMEM((2, 64, 384), BF),
            pltpu.VMEM((2, 64, 384), BF),
            pltpu.VMEM((49, 8, 256), F32),
            pltpu.VMEM((4, 256, 256), BF),
            pltpu.VMEM((16, 32, 256), F32),
            pltpu.VMEM((7, 16, 16, 256), F32),
            pltpu.VMEM((8, 3, 32, 256), F32),
            pltpu.VMEM((16, 16, 16, 256), F32),
            pltpu.VMEM((512, 256), BF),
            pltpu.VMEM((512, 256), BF),
            pltpu.VMEM((256, 256), BF),
            pltpu.VMEM((256, 128), BF),
            pltpu.VMEM((256, 512), BF),
            pltpu.VMEM((16, 1024), F32),
            pltpu.VMEM((256, 512), BF),
            pltpu.VMEM((16, 128, 384), BF),
            pltpu.VMEM((16, 384, 256), BF),
            pltpu.VMEM((128, 256), BF),
            pltpu.VMEM((128, 1024), BF),
            pltpu.VMEM((2, 1024, 256), F32),
            pltpu.VMEM((2, 3, 128, 256), BF),
            pltpu.VMEM((4, 128, 384), BF),
            pltpu.VMEM((4, 384, 128), BF),
            dma((2, 2, 2, 3)), dma((2, 2, 2, 3)),
            dma((11,)), dma((11,)),
            dma((7,)), dma((7,)),
            dma((9,)), dma((9,)),
            dma((16,)), dma((16,)),
        ],
        compiler_params=pltpu.CompilerParams(
            collective_id=0, has_side_effects=True, vmem_limit_bytes=60 * 1024 * 1024),
    )(
        air_member_values, marine_member_values.reshape(16, 256, 256), water_cell_indicator,
        initial_air_filter, initial_filter_offset.reshape(1, 256),
        later_air_filter, later_filter_offset.reshape(1, 256),
        air_to_exchange_matrix.T, exchange_to_marine_matrix, marine_wide_filter,
        wide_filter_offset.reshape(1, 256), marine_rescale_factor.reshape(1, 256),
        hidden_entry_matrix, hidden_entry_offset.reshape(1, 1024), hidden_exit_matrix,
        marine_to_skin_matrix.T, skin_to_air_matrix, *cell_tables(),
        air_neighbour_faces.T, marine_neighbour_faces.T, marine_spanned_quarter, places,
    )
    return atm_next, advanced.reshape(1, 16, 256, 256)


def solution(mesh):
    in_specs = (
        P("ocn", "atm", None, None),
        P("atm", "ocn", None, None),
        P(),
        P(),
        P(),
        P("ocn", None),
    ) + (P(),) * 14
    out_specs = (P("ocn", "atm", None, None), P("atm", "ocn", None, None))
    return jax.shard_map(
        on_device, mesh=mesh, in_specs=in_specs, out_specs=out_specs, check_vma=False
    )
```

```python
import jax
import jax.numpy as jnp
import numpy as np
from jax import lax
from jax.experimental import pallas as pl
from jax.experimental.pallas import tpu as pltpu
from jax.sharding import PartitionSpec as P

BF = jnp.bfloat16
F32 = jnp.float32
MESH = pl.DeviceIdType.MESH
VMEM = pl.BlockSpec(memory_space=pltpu.VMEM)
SMEM = pl.BlockSpec(memory_space=pltpu.SMEM)
HBM = pl.BlockSpec(memory_space=pl.ANY)
C0 = 0.7978845608028654
C1 = C0 * 0.044715


def gelu(x):
    half = 0.5 * x
    return half + half * jnp.tanh(x * (C0 + C1 * (x * x)))


def dot(a, b):
    return jnp.dot(a, b, preferred_element_type=F32)


def dot_t(a, b):
    return lax.dot_general(a, b, (((0,), (0,)), ((), ())), preferred_element_type=F32)


def cell_tables():
    split = np.zeros((256, 256), np.float32)
    join = np.zeros((256, 256), np.float32)
    for r in range(16):
        for q in range(16):
            a, b = r // 8, q // 8
            cell = (r % 8) * 8 + q % 8
            split[r * 16 + q, b * 128 + a * 64 + cell] = 1
            join[a * 128 + b * 64 + cell, r * 16 + q] = 1
    air_rim = np.zeros((64, 256), np.float32)
    for c in range(16):
        for kind, cell in enumerate((c, 240 + c, c * 16, c * 16 + 15)):
            air_rim[kind * 16 + c, cell] = 1
    ocean_rim = np.zeros((160, 256), np.float32)
    side_sel = np.zeros((2, 48, 160), np.float32)
    for j in range(3):
        for c in range(16):
            ocean_rim[j * 16 + c, j * 16 + c] = 1
            ocean_rim[48 + j * 16 + c, (13 + j) * 16 + c] = 1
            for side, (col, start) in enumerate(((13 + j, 128), (j, 96))):
                at = start + (c - 3) * 3 + j
                if c < 3:
                    at = c * 16 + col
                elif c >= 13:
                    at = 48 + (c - 13) * 16 + col
                else:
                    ocean_rim[at, c * 16 + col] = 1
                side_sel[side, j * 16 + c, at] = 1
    strip = np.zeros((4, 256, 128), np.float32)
    for c in range(16):
        for side, cell in enumerate((240 + c, c, c * 16 + 15, c * 16)):
            strip[side, :, side * 16 + c] = join[:, cell]
    up = np.zeros((128, 256), np.float32)
    for r in range(16):
        for q in range(16):
            up[(r // 2) * 8 + q // 2, r * 16 + q] = 1
    pick = np.zeros((4, 256, 256), np.float32)
    for j in range(3):
        for c in range(16):
            cells = ((13 + j) * 16 + c, j * 16 + c, c * 16 + 13 + j, c * 16 + j)
            for side, cell in enumerate(cells):
                pick[side, cell, side * 64 + j * 16 + c] = 1
    up_rim = np.einsum("qc,scd->sqd", up, pick)
    shift = np.zeros((512, 7, 384), np.float32)
    for j in range(7):
        for q in range(16):
            col = q + j
            for r in range(22):
                at = r * 16 + q
                if 3 <= r < 19 and 3 <= col < 19:
                    shift[(r - 3) * 16 + col - 3, j, at] = 1
                elif 3 <= col < 19:
                    side, k = (0, r) if r < 3 else (1, r - 19)
                    shift[256 + side * 64 + k * 16 + col - 3, j, at] = 1
                elif 3 <= r < 19:
                    side, k = (2, col) if col < 3 else (3, col - 19)
                    shift[256 + side * 64 + k * 16 + r - 3, j, at] = 1
    shift_air = np.zeros((384, 3, 384), np.float32)
    for j in range(3):
        for q in range(16):
            col = q + j
            for r in range(18):
                at = r * 16 + q
                if 1 <= r < 17 and 1 <= col < 17:
                    shift_air[(r - 1) * 16 + col - 1, j, at] = 1
                elif 1 <= col < 17:
                    shift_air[256 + (0 if r < 1 else 16) + col - 1, j, at] = 1
                elif 1 <= r < 17:
                    shift_air[256 + (32 if col < 1 else 48) + r - 1, j, at] = 1
    mean = np.zeros((2, 256, 128), np.float32)
    for r in range(16):
        for q in range(16):
            for h in range(2):
                mean[h, r * 16 + q, h * 64 + (r // 2) * 8 + q // 2] = 0.25
    tables = (
        split,
        join,
        air_rim,
        ocean_rim,
        side_sel,
        strip.reshape(1024, 128),
        up,
        up_rim.reshape(512, 256),
        pick.reshape(1024, 256),
        shift.reshape(512, 2688),
        shift_air.reshape(384, 1152),
        mean,
    )
    return tuple(jnp.asarray(table, BF) for table in tables)


def coordinates():
    a = lax.axis_index("atm")
    o = lax.axis_index("ocn")
    return a, o, lax.div(a, 4), lax.rem(a, 4)


def axis_partner(mm, phase, d):
    a, o, x, z = coordinates()
    if (mm + phase) % 2 == 0:
        place = lax.rem(z + d, 4)
        return (x * 4 + place, o), place
    place = lax.rem(x + d, 4)
    return (place * 4 + z, o), place


def coupling_partner(k):
    a, o, x, z = coordinates()
    return 2 * o + k, lax.div(a, 2)


def is_me(k):
    a, o, x, z = coordinates()
    return jnp.logical_and(lax.div(a, 2) == o, lax.rem(a, 2) == k)


def remote(src, dst, send, recv, target):
    return pltpu.make_async_remote_copy(
        src_ref=src, dst_ref=dst, send_sem=send, recv_sem=recv,
        device_id=target, device_id_type=MESH)


def greet():
    barrier = pltpu.get_barrier_semaphore()
    a, o, x, z = coordinates()

    def signal(target):
        pl.semaphore_signal(barrier, inc=1, device_id=target, device_id_type=MESH)

    for d in (1, 2, 3):
        for mm in range(2):
            signal(axis_partner(mm, 0, d)[0])
    for d in range(1, 8):
        signal((a, lax.rem(o + d, 8)))
    for k in range(2):
        @pl.when(jnp.logical_not(is_me(k)))
        def _():
            signal(coupling_partner(k))


def await_greetings():
    a, o, x, z = coordinates()
    pl.semaphore_wait(pltpu.get_barrier_semaphore(), 15 - jnp.where(lax.div(a, 2) == o, 1, 0))


def rim_exchange(rd, tiles, nbr, air_rim, g1, st, r2, send, recv):
    a, o, x, z = coordinates()

    def first_copy(mm, d):
        here = axis_partner(mm, 0, 0)[1]
        part = g1[rd][mm].at[here]
        return remote(part, part, send.at[rd, 0, mm, d - 1], recv.at[rd, 0, mm, d - 1],
                      axis_partner(mm, 0, d)[0])

    def second_copy(mm, d):
        here = axis_partner(mm, 1, 0)[1]
        return remote(st.at[rd, mm, d - 1], r2[rd][mm].at[here], send.at[rd, 1, mm, d - 1],
                      recv.at[rd, 1, mm, d - 1], axis_partner(mm, 1, d)[0])

    def begin(mm):
        here = axis_partner(mm, 0, 0)[1]

        @pl.loop(0, 4, unroll=4)
        def _(k):
            rims = dot(air_rim[...], tiles[mm, k]).astype(BF).reshape(4, 16, 256)
            g1[rd][mm][here, pl.ds(k * 4, 4)] = rims

    def send_first(mm):
        for d in (1, 3, 2):
            first_copy(mm, d).start()

    def middle():
        for mm in range(2):
            for d in (1, 2, 3):
                first_copy(mm, d).wait_recv()
            for d in (2, 1, 3, 0):
                (dest, _), place = axis_partner(mm, 1, d)

                @pl.loop(0, 16, unroll=4)
                def _(slot):
                    n = nbr[lax.rem(slot, 4), dest * 4 + lax.div(slot, 4)]
                    owner = lax.div(n, 4)
                    from_place = lax.rem(owner, 4) if mm == 0 else lax.div(owner, 4)
                    side = lax.rem(slot, 4)
                    kind = side + 1 - 2 * lax.rem(side, 2)
                    strip = g1[rd][mm][from_place, lax.rem(n, 4) * 4 + kind]
                    if d == 0:
                        r2[rd][mm][place, slot] = strip
                    else:
                        st[rd, mm, d - 1, slot] = strip

                if d > 0:
                    second_copy(mm, d).start()

    def finish():
        for mm in range(2):
            for d in (1, 2, 3):
                second_copy(mm, d).wait_recv()
        for mm in range(2):
            for d in (1, 2, 3):
                first_copy(mm, d).wait_send()
                second_copy(mm, d).wait_send()

    def strip_of(mm, slot):
        n = nbr[lax.rem(slot, 4), a * 4 + lax.div(slot, 4)]
        owner = lax.div(n, 4)
        place = lax.div(owner, 4) if mm == 0 else lax.rem(owner, 4)
        return r2[rd][mm][place, slot]

    return begin, middle, finish, strip_of, send_first


def stage_tile(k, tile, strips, pad, shifted):
    pad[1:17, 8:24, :] = tile.astype(F32).reshape(16, 16, 256)
    pad[0, 8:24, :] = strips[0].astype(F32)
    pad[17, 8:24, :] = strips[1].astype(F32)
    pad[1:17, 7, :] = strips[2].astype(F32)
    pad[1:17, 24, :] = strips[3].astype(F32)
    for j in range(3):
        shifted[j, k] = pad[:, 7 + j : 23 + j, :].astype(BF).reshape(288, 256)


def convolve(shifted, filt):
    total = None
    for offset in range(9):
        i, j = divmod(offset, 3)
        part = dot(shifted[j, :, i * 16 : i * 16 + 256, :].reshape(1024, 256), filt[offset])
        total = part if total is None else total + part
    return total


def interior(tile, wide, bias, pad, moved, depth):
    pad[:, 8:24, :] = tile
    for j in range(7):
        moved[j] = pad[:, 5 + j : 21 + j, :]
    for g in range(2):
        lanes = slice(g * 128, g * 128 + 128)
        start = jnp.broadcast_to(bias[:, lanes], (8, 128))
        for c in (0, 8):
            total = [start] * 16
            for j in range(7):
                rows = [moved[j, r, c : c + 8, lanes] for r in range(16)]
                weights = [wide[i * 7 + j, :, lanes] for i in range(7)]
                for p in range(16):
                    for i in range(7):
                        if 0 <= p + i - 3 < 16:
                            total[p] = total[p] + rows[p + i - 3] * weights[i]
            for p in range(16):
                depth[p, c : c + 8, lanes] = total[p]


def rim_sums(side, strip, wide, pad):
    pad[:, 8:24, :] = strip
    total = [None] * 3
    for shift in range(7):
        part = pad[:, 5 + shift : 21 + shift, :].reshape(3, 2, 8, 256)
        for place in range(3):
            for k in range(3):
                along = k - place if side in (0, 2) else 6 + k - place
                if not 0 <= along < 7 or (k < place) == (side in (0, 2)) and k != place:
                    continue
                i, j = (along, shift) if side < 2 else (shift, along)
                term = part[k] * wide[i * 7 + j][None]
                total[place] = term if total[place] is None else total[place] + term
    return [value.reshape(16, 256) for value in total]


def kernel(air_far, marine_far, sea, filt_a_far, bias_a, filt_b_far, bias_b, flux_t, exchange, wide_in,
           wide_bias, gain, entry_far, entry_bias, leave_far, skin_t, back,
           split, join, air_rim, ocean_rim, side_sel, strip_far, up, up_rim_far, pick_far, shift_far, shift_air_far, mean,
           air_nbr, ocean_nbr, quarter, places,
           result, advanced,
           filt_a, filt_b, entry, leave, shift, air, marine, strip_sel, up_rim, pick, shift_air, fetch,
           first, pad_a, shifted, g00, g01, g10, g11, st, r00, r01, r10, r11,
           rims, sea_all, wet32, flux_own, flux_in, skin_in, back_out, back_in,
           wide, weights, pad_o, moved, pad_r, depth, normed_even, normed_odd, fine_flux,
           fluxes, rim_flux, rim_sea, cells, columns, im2col, centre_q, rim_q,
           sums, field_weights, field_columns, field_cells,
           asend, arecv, bsend, brecv, ssend, srecv, fsend, frecv, ksend, krecv):
    a, o, x, z = coordinates()
    g1 = ((g00, g01), (g10, g11))
    r2 = ((r00, r01), (r10, r11))
    right = (a, lax.rem(o + 2, 8))
    left = (a, lax.rem(o + 6, 8))
    twin = (a, o + 1 - 2 * lax.rem(o, 2))
    before = lax.rem(o + 6, 8)
    after = lax.rem(o + 2, 8)
    across = lax.rem(o + 4, 8)
    lane = lax.broadcasted_iota(jnp.int32, (16, 128), 1)
    share = jnp.full((16, 256), 0.0625, BF)

    def sea_columns(t):
        row = jnp.broadcast_to(sea[pl.ds(t, 1), :].astype(F32), (16, 256)).astype(BF)
        return dot_t(row, share)

    def rim_copy(block, half, target, n):
        part = rims.at[block, pl.ds(half * 8, 8)]
        return remote(part, part, bsend.at[n], brecv.at[n], target)

    def block_copy(block, n):
        return remote(rims.at[block], rims.at[block], bsend.at[n], brecv.at[n], twin)

    own_copies = [rim_copy(o, 0, right, 0), rim_copy(o, 1, left, 1),
                  rim_copy(o, 1, right, 2), rim_copy(o, 0, left, 3)]
    onward_right = rim_copy(before, 0, right, 4)
    onward_left = rim_copy(after, 1, left, 5)
    twin_copies = [block_copy(o, 6), block_copy(before, 7), block_copy(after, 8),
                   rim_copy(across, 0, twin, 9), rim_copy(across, 1, twin, 10)]

    def sea_copy(d):
        return remote(sea_all.at[o], sea_all.at[o], ssend.at[d - 1], srecv.at[d - 1],
                      (a, lax.rem(o + d, 8)))

    def flux_copy(d):
        part = flux_in.at[pl.ds(8 * o, 8)]
        return remote(part, part, fsend.at[d + 1], frecv.at[d + 1], (a, lax.rem(o + d, 8)))

    def skin_copy(d, half):
        part = skin_in.at[o, pl.ds(half * 4, 4)]
        n = d + 1 + 7 * half
        return remote(part, part, ksend.at[n], krecv.at[n], (a, lax.rem(o + d, 8)))

    def first_flux(k):
        return remote(flux_own.at[k], flux_in.at[pl.ds(4 * a, 4)], fsend.at[k], frecv.at[lax.rem(a, 2)],
                      coupling_partner(k))

    def last_skin(k):
        return remote(back_out.at[k], back_in.at[lax.rem(a, 2)], ksend.at[k],
                      krecv.at[lax.rem(a, 2)], coupling_partner(k))

    def unless_me(k, act):
        pl.when(jnp.logical_not(is_me(k)))(act)

    greet()
    fetches = [
        pltpu.make_async_copy(far, near, fetch.at[n])
        for n, (far, near) in enumerate((
            (filt_a_far, filt_a), (shift_far, shift), (entry_far, entry), (leave_far, leave),
            (filt_b_far, filt_b), (air_far, air), (marine_far, marine), (strip_far, strip_sel),
            (up_rim_far, up_rim), (pick_far, pick), (shift_air_far, shift_air)))
    ]
    for n in (5, 6, 0, 1, 2, 3, 4, 7, 8, 9, 10):
        fetches[n].start()
    fetches[5].wait()
    air_first = rim_exchange(0, air, air_nbr, air_rim, g1, st, r2, asend, arecv)
    air_second = rim_exchange(1, first, air_nbr, air_rim, g1, st, r2, asend, arecv)
    air_first[0](0)
    air_first[0](1)
    sea_all[o] = sea[...].astype(F32).astype(BF)
    fetches[6].wait()

    @pl.loop(0, 16, unroll=4)
    def _(t):
        wet = (ocean_rim[...].astype(F32) * sea[pl.ds(t, 1), :].astype(F32)).astype(BF)
        rims[o, t] = dot(wet, marine[t]).astype(BF)

    await_greetings()
    air_first[4](0)
    air_first[4](1)
    for copy in own_copies:
        copy.start()
    twin_copies[0].start()
    for d in range(1, 8):
        sea_copy(d).start()

    spread_in = exchange[...].astype(F32)
    weights[...] = jnp.zeros(weights.shape, BF)
    for i in range(7):
        for j in range(7):
            row = wide_in[i * 7 + j : i * 7 + j + 1, :].astype(F32)
            wide[i * 7 + j] = jnp.broadcast_to(row, (8, 256))
            at = (i % 2) * 128 + j * 16
            weights[i // 2, at : at + 16, :] = (spread_in * row).astype(BF)
    pad_o[...] = jnp.zeros(pad_o.shape, F32)
    pad_r[...] = jnp.zeros(pad_r.shape, F32)
    pad_a[...] = jnp.zeros(pad_a.shape, F32)

    def interiors(low, high):
        @pl.loop(low, high)
        def _(t):
            tile = (marine[t].astype(F32) * sea_columns(t)).reshape(16, 16, 256)
            interior(tile, wide, wide_bias, pad_o, moved, depth.at[t])

    interiors(0, 5)
    for n in (7, 8, 9, 10):
        fetches[n].wait()
    air_first[1]()
    interiors(5, 11)
    air_first[2]()
    fetches[0].wait()

    for mm in range(2):
        @pl.loop(0, 4)
        def _(k):
            strips = [air_first[3](mm, k * 4 + s) for s in range(4)]
            stage_tile(k, air[mm, k], strips, pad_a, shifted)

        first[mm] = (air[mm].astype(F32).reshape(1024, 256)
                     + gelu(convolve(shifted, filt_a) + bias_a[...])).astype(BF).reshape(4, 256, 256)

        @pl.loop(0, 4)
        def _(k):
            flux = lax.dot_general(flux_t[...], first[mm, k], (((1,), (1,)), ((), ())),
                                   preferred_element_type=F32).astype(BF)
            quads = dot(flux, split[...])
            low = lax.rem(places[a * 8 + k * 2], 2)
            high = lax.rem(places[a * 8 + k * 2 + 1], 2)
            chosen = jnp.where(lane < 64, low, high)
            flux_own[mm, k] = jnp.where(
                chosen == 1, quads[:, 128:], quads[:, :128]).astype(BF)

        unless_me(mm, lambda: first_flux(mm).start())

        @pl.when(is_me(mm))
        def _():
            flux_in[pl.ds(4 * a, 4)] = flux_own[mm]

        air_second[0](mm)
        air_second[4](mm)

    interiors(11, 14)
    for k in range(2):
        def arrival():
            remote(flux_own.at[0], flux_in.at[pl.ds(8 * o + 4 * k, 4)], fsend.at[k], frecv.at[k],
                   coupling_partner(k)).wait_recv()
        unless_me(k, arrival)
    for d in range(1, 8):
        flux_copy(d).start()
    own_copies[0].wait_recv()
    onward_right.start()
    own_copies[1].wait_recv()
    onward_left.start()
    interiors(14, 16)
    air_second[1]()
    for d in range(1, 8):
        sea_copy(d).wait_recv()
    wet32[...] = sea_all[...].astype(F32).reshape(128, 1, 256)
    for d in range(1, 8):
        flux_copy(d).wait_recv()
    own_copies[2].wait_recv()
    twin_copies[1].start()
    own_copies[3].wait_recv()
    twin_copies[2].start()

    def quadrant(tile):
        q = quarter[tile]
        both = flux_in[lax.div(q, 4)].astype(F32)
        upper = lax.rem(lax.div(q, 2), 2)
        turned = jnp.where(upper == 1, pltpu.roll(both, 64, 1), both)
        return jnp.where(lane < 64, turned, 0.0).astype(BF)

    @pl.loop(0, 16)
    def _(t):
        rows = pl.ds(pl.multiple_of(t * 16, 16), 16)
        fluxes[rows, :] = quadrant(o * 16 + t)
        for s in range(4):
            n = ocean_nbr[s, o * 16 + t]
            rim_flux[rows, s * 128 : (s + 1) * 128] = quadrant(n)
            rim_sea[pl.ds(t, 1), s * 256 : (s + 1) * 256] = wet32[n]

    fine = dot(fluxes[...], up[...])
    sea_here = jnp.broadcast_to(sea[...].astype(F32).reshape(16, 1, 256), (16, 16, 256))
    cells[:, 0:256] = (fine * sea_here.reshape(256, 256)).astype(BF)
    rim_wet = dot(rim_sea[...].astype(BF), pick[...])
    rim_wet = jnp.broadcast_to(rim_wet.reshape(16, 1, 256), (16, 16, 256)).reshape(256, 256)
    cells[:, 256:512] = (dot(rim_flux[...], up_rim[...]) * rim_wet).astype(BF)
    fine_flux[...] = fine.astype(BF)

    fetches[1].wait()
    columns[:, 112:128, :] = jnp.zeros((16, 16, 384), BF)
    for j in range(7):
        shifts = dot(cells[...], shift[:, j * 384 : j * 384 + 384]).astype(BF)
        columns[:, j * 16 : j * 16 + 16, :] = shifts.reshape(16, 16, 384)

    @pl.loop(0, 16)
    def _(t):
        turned = columns[t].astype(F32).T.astype(BF)
        im2col[t, :, 0:128] = turned
        im2col[t, 0:368, 128:256] = turned[16:384]
        im2col[t, 368:384, 128:256] = jnp.zeros((16, 128), BF)

    @pl.loop(0, 4)
    def _(p):
        four = pl.ds(p * 4, 4)
        total = depth[four].reshape(1024, 256)
        for i in range(4):
            total = total + dot(im2col[four, i * 32 : i * 32 + 256, :].reshape(1024, 256),
                                weights[i])
        depth[four] = total.reshape(4, 16, 16, 256)

    def early_sums(mm):
        @pl.loop(0, 4)
        def _(k):
            strips = [air_second[3](mm, k * 4 + s) for s in range(4)]
            stage_tile(k, first[mm, k], strips, pad_a, shifted)

        sums[mm] = convolve(shifted, filt_b)

    fetches[4].wait()
    field_weights[...] = jnp.zeros(field_weights.shape, BF)
    for h in range(2):
        for i in range(3):
            for j in range(3):
                at = h * 64 + j * 16
                field_weights[h, i, at : at + 16] = dot(back[...], filt_b[3 * i + j]).astype(BF)
    field_columns[...] = jnp.zeros(field_columns.shape, BF)

    onward_right.wait_recv()
    twin_copies[3].start()
    onward_left.wait_recv()
    twin_copies[4].start()
    fetches[2].wait()
    fetches[3].wait()
    leave[...] = (leave[...].astype(F32) * 0.5).astype(BF)
    for copy in twin_copies:
        copy.wait_recv()

    def add_rim(t, h, s):
        n = ocean_nbr[s, o * 16 + t]
        beside = rims[lax.div(n, 16), lax.rem(n, 16)]
        if s < 2:
            strip = beside[48 - 48 * s : 96 - 48 * s].astype(F32)
        else:
            strip = dot(side_sel[s - 2], beside)
        sums = rim_sums(s, strip.reshape(3, 16, 256), wide, pad_r.at[h * 4 + s])
        for place in range(3):
            if s < 2:
                row = place + 13 * s
                depth[t, row] = depth[t, row] + sums[place]
            else:
                col = place + 13 * (s - 2)
                depth[t, :, col, :] = depth[t, :, col, :] + sums[place]

    def norm(t, h, normed):
        value = depth[t].reshape(256, 256)
        value = value - jnp.mean(value, axis=1, keepdims=True)
        spread = jnp.mean(value * value, axis=1, keepdims=True)
        value = value * lax.rsqrt(spread + 1e-6) * gain[...]
        normed[h * 256 : h * 256 + 256] = value.astype(BF)

    def emit(p, outer):
        pair = jnp.zeros((16, 128), F32)
        for h in range(2):
            t = p * 2 + h
            rows = pl.ds(pl.multiple_of(t * 16, 16), 16)
            forced = marine[t].astype(F32) + dot_t(fine_flux[rows, :], exchange[...])
            whole = forced + outer[h * 256 : h * 256 + 256]
            done = (sea_columns(t) * whole).astype(BF)
            advanced[t] = done
            surface = lax.dot_general(skin_t[...], done, (((1,), (1,)), ((), ())),
                                      preferred_element_type=F32).astype(BF)
            pair = pair + dot(surface, mean[h])
        skin_in[o, p] = pair.astype(BF)

    def work(p, now, later):
        outer = None
        for part in range(4):
            if now is not None:
                lanes = slice(part * 256, part * 256 + 256)
                inner = dot(now[...], entry[:, lanes]) + entry_bias[:, lanes]
                inner = (inner + inner * jnp.tanh(inner * (C0 + C1 * (inner * inner)))).astype(BF)
                term = dot(inner, leave[lanes, :])
                outer = term if outer is None else outer + term
            if later is not None:
                for h, s in ((part // 2, part % 2 * 2), (part // 2, part % 2 * 2 + 1)):
                    add_rim(p * 2 + 2 + h, h, s)
        if later is not None:
            for h in range(2):
                norm(p * 2 + 2 + h, h, later)
        if now is not None:
            emit(p, outer)

    even, odd = normed_even, normed_odd
    work(jnp.int32(-1), None, even)

    @pl.loop(0, 3)
    def _(q):
        work(2 * q, even, odd)
        work(2 * q + 1, odd, even)

    for d in range(1, 8):
        skin_copy(d, 0).start()
    work(jnp.int32(6), even, odd)
    work(jnp.int32(7), odd, None)

    for d in range(1, 8):
        skin_copy(d, 1).start()
    air_second[2]()
    early_sums(0)

    for d in range(1, 8):
        skin_copy(d, 0).wait_recv()
        skin_copy(d, 1).wait_recv()

    def half(j):
        s = lax.div(places[j], 2)
        b = lax.rem(places[j], 2)
        both = skin_in[lax.div(s, 16), lax.div(lax.rem(s, 16), 2)].astype(F32)
        turned = jnp.where(lax.rem(s, 2) == b, both, pltpu.roll(both, 64, 1))
        inside = jnp.where(lane < 64, 0, 1) == b
        return jnp.where(inside, turned, 0.0).astype(BF)

    @pl.loop(0, 8, unroll=4)
    def _(k):
        rows = pl.ds(pl.multiple_of(k * 16, 16), 16)
        tile = o * 8 + k
        for h in range(2):
            centre_q[rows, h * 128 : h * 128 + 128] = half(tile * 2 + h)
            for s in range(4):
                n = air_nbr[s, tile]
                at = s * 256 + h * 128
                rim_q[rows, at : at + 128] = half(n * 2 + h)

    centre = dot(centre_q[...], join[...]).astype(BF)
    rim = dot(rim_q[...], strip_sel[...]).astype(BF)
    for k in range(2):
        back_out[k, :, 0:256] = centre[k * 64 : k * 64 + 64]
        back_out[k, :, 256:384] = rim[k * 64 : k * 64 + 64]
        unless_me(k, lambda: last_skin(k).start())

        @pl.when(is_me(k))
        def _():
            back_in[k] = back_out[k]

    early_sums(1)
    for mm in range(2):
        def arrival():
            remote(back_out.at[0], back_in.at[mm], ksend.at[mm], krecv.at[mm],
                   coupling_partner(mm)).wait_recv()
        unless_me(mm, arrival)

    for j in range(3):
        moved_fields = dot(back_in[...].reshape(128, 384), shift_air[:, j * 384 : j * 384 + 384])
        moved_fields = moved_fields.astype(BF).reshape(4, 2, 16, 384)
        for h in range(2):
            at = h * 64 + j * 16
            field_columns[:, at : at + 16, :] = moved_fields[:, h]
    for p in range(4):
        field_cells[p] = field_columns[p].astype(F32).T.astype(BF)
    for mm in range(2):
        parts = []
        for h in range(2):
            total = None
            for i in range(3):
                rows = field_cells[2 * mm : 2 * mm + 2, i * 16 : i * 16 + 256, :]
                term = dot(rows.reshape(512, 128), field_weights[h, i])
                total = term if total is None else total + term
            parts.append(total.reshape(2, 256, 256))
        for k in range(4):
            rows = slice(k * 16, k * 16 + 16)
            add = dot_t(back_in[mm, rows, 0:256], back[...])
            tile = (first[mm, k].astype(F32) + add).astype(BF).astype(F32)
            total = sums[mm, k * 256 : k * 256 + 256] + parts[k % 2][k // 2] + bias_b[...]
            result[mm, k] = (tile + gelu(total)).astype(BF)

    for copy in own_copies + [onward_right, onward_left] + twin_copies:
        copy.wait_send()
    for d in range(1, 8):
        sea_copy(d).wait_send()
        flux_copy(d).wait_send()
        skin_copy(d, 0).wait_send()
        skin_copy(d, 1).wait_send()
    for k in range(2):
        unless_me(k, lambda: first_flux(k).wait_send())
        unless_me(k, lambda: last_skin(k).wait_send())


def on_device(
    air_member_values,
    marine_member_values,
    air_neighbour_faces,
    marine_neighbour_faces,
    marine_spanned_quarter,
    water_cell_indicator,
    initial_air_filter,
    initial_filter_offset,
    later_air_filter,
    later_filter_offset,
    air_to_exchange_matrix,
    exchange_to_marine_matrix,
    marine_wide_filter,
    wide_filter_offset,
    marine_rescale_factor,
    hidden_entry_matrix,
    hidden_entry_offset,
    hidden_exit_matrix,
    marine_to_skin_matrix,
    skin_to_air_matrix,
):
    index = lax.broadcasted_iota(jnp.int32, (128, 128), 0)
    tile = lax.broadcasted_iota(jnp.int32, (128, 128), 1)
    covered = jnp.broadcast_to(marine_spanned_quarter[None, :], (128, 128))
    code = jnp.where(covered == 2 * index, 2 * tile, 0)
    code = jnp.where(covered == 2 * index + 1, 2 * tile + 1, code)
    places = jnp.sum(code, axis=1)
    strips = pltpu.VMEM((4, 16, 16, 256), BF)
    dma = pltpu.SemaphoreType.DMA
    atm_next, advanced = pl.pallas_call(
        kernel,
        out_shape=(
            jax.ShapeDtypeStruct((2, 4, 256, 256), BF),
            jax.ShapeDtypeStruct((16, 256, 256), BF),
        ),
        in_specs=[HBM, HBM, VMEM, HBM, VMEM, HBM] + [VMEM] * 6 + [HBM, VMEM, HBM] + [VMEM] * 7
        + [HBM, VMEM] + [HBM] * 4 + [VMEM] + [SMEM] * 4,
        out_specs=(VMEM, VMEM),
        scratch_shapes=[
            pltpu.VMEM((9, 256, 256), BF),
            pltpu.VMEM((9, 256, 256), BF),
            pltpu.VMEM((256, 1024), BF),
            pltpu.VMEM((1024, 256), BF),
            pltpu.VMEM((512, 2688), BF),
            pltpu.VMEM((2, 4, 256, 256), BF),
            pltpu.VMEM((16, 256, 256), BF),
            pltpu.VMEM((1024, 128), BF),
            pltpu.VMEM((512, 256), BF),
            pltpu.VMEM((1024, 256), BF),
            pltpu.VMEM((384, 1152), BF),
            dma((11,)),
            pltpu.VMEM((2, 4, 256, 256), BF),
            pltpu.VMEM((18, 32, 256), F32),
            pltpu.VMEM((3, 4, 288, 256), BF),
            strips, strips, strips, strips,
            pltpu.VMEM((2, 2, 3, 16, 16, 256), BF),
            strips, strips, strips, strips,
            pltpu.VMEM((8, 16, 160, 256), BF),
            pltpu.VMEM((8, 16, 256), BF),
            pltpu.VMEM((128, 1, 256), F32),
            pltpu.VMEM((2, 4, 16, 128), BF),
            pltpu.VMEM((64, 16, 128), BF),
            pltpu.VMEM((8, 8, 16, 128), BF),
            pltpu.VMEM((2, 64, 384), BF),
            pltpu.VMEM((2, 64, 384), BF),
            pltpu.VMEM((49, 8, 256), F32),
            pltpu.VMEM((4, 256, 256), BF),
            pltpu.VMEM((16, 32, 256), F32),
            pltpu.VMEM((7, 16, 16, 256), F32),
            pltpu.VMEM((8, 3, 32, 256), F32),
            pltpu.VMEM((16, 16, 16, 256), F32),
            pltpu.VMEM((512, 256), BF),
            pltpu.VMEM((512, 256), BF),
            pltpu.VMEM((256, 256), BF),
            pltpu.VMEM((256, 128), BF),
            pltpu.VMEM((256, 512), BF),
            pltpu.VMEM((16, 1024), F32),
            pltpu.VMEM((256, 512), BF),
            pltpu.VMEM((16, 128, 384), BF),
            pltpu.VMEM((16, 384, 256), BF),
            pltpu.VMEM((128, 256), BF),
            pltpu.VMEM((128, 1024), BF),
            pltpu.VMEM((2, 1024, 256), F32),
            pltpu.VMEM((2, 3, 128, 256), BF),
            pltpu.VMEM((4, 128, 384), BF),
            pltpu.VMEM((4, 384, 128), BF),
            dma((2, 2, 2, 3)), dma((2, 2, 2, 3)),
            dma((11,)), dma((11,)),
            dma((7,)), dma((7,)),
            dma((9,)), dma((9,)),
            dma((16,)), dma((16,)),
        ],
        compiler_params=pltpu.CompilerParams(
            collective_id=0, has_side_effects=True, vmem_limit_bytes=60 * 1024 * 1024),
    )(
        air_member_values, marine_member_values.reshape(16, 256, 256), water_cell_indicator,
        initial_air_filter, initial_filter_offset.reshape(1, 256),
        later_air_filter, later_filter_offset.reshape(1, 256),
        air_to_exchange_matrix.T, exchange_to_marine_matrix, marine_wide_filter,
        wide_filter_offset.reshape(1, 256), marine_rescale_factor.reshape(1, 256),
        hidden_entry_matrix, hidden_entry_offset.reshape(1, 1024), hidden_exit_matrix,
        marine_to_skin_matrix.T, skin_to_air_matrix, *cell_tables(),
        air_neighbour_faces.T, marine_neighbour_faces.T, marine_spanned_quarter, places,
    )
    return atm_next, advanced.reshape(1, 16, 256, 256)


def solution(mesh):
    in_specs = (
        P("ocn", "atm", None, None),
        P("atm", "ocn", None, None),
        P(),
        P(),
        P(),
        P("ocn", None),
    ) + (P(),) * 14
    out_specs = (P("ocn", "atm", None, None), P("atm", "ocn", None, None))
    return jax.shard_map(
        on_device, mesh=mesh, in_specs=in_specs, out_specs=out_specs, check_vma=False
    )
```
